32 devices in a mesh: rep: 2 (over y), wide: 8 (over z, x), tensor: 2 (over core).
Axes of the slice: x: 2, y: 2, z: 4, core: 2. Of those that a mesh axis runs over, the one named last changes fastest.
Arguments:
- tokens: bfloat16 [128, 8192], P(('rep', 'wide')), parts along dimension 0, may hold values from -6 to 6
- query_quant_codes: int32 [8192, 8192], P(None, ('tensor', 'wide')), may hold values from 0 to 15
- query_absmax_scale: float32 [128, 8192], P(None, ('tensor', 'wide')), may hold values from 0.012153398 to 0.039774757
- output_quant_codes: int32 [8192, 8192], P('tensor', 'wide'), may hold values from 0 to 15
- output_absmax_scale: float32 [128, 8192], P('tensor', 'wide'), may hold values from 0.03314563 to 0.13258252
- adapter_down_maps: bfloat16 [8192, 48, 32], P(None, 'wide'), may hold values from -0.0625 to 0.0625
- adapter_up_maps: bfloat16 [48, 32, 8192], P('wide', None, 'tensor'), may hold values from -1 to 1
- row_adapter_index: int32 [128], P('rep'), parts along dimension 0, may hold values from 0 to 47
- adapter_storage_slot: int32 [48], replicated, may hold values from 0 to 47, each once
- row_cache_length: int32 [128], P(('rep', 'wide')), parts along dimension 0, may hold values from 2 to 64
- stored_key_cache: bfloat16 [128, 64, 1024], P(('rep', 'wide'), None, 'tensor'), parts along dimension 0, may hold values from -201 to 201
- stored_value_cache: bfloat16 [128, 64, 1024], P(('rep', 'wide'), None, 'tensor'), parts along dimension 0, may hold values from -6 to 6
- fresh_token_key: bfloat16 [128, 1024], P(('rep', 'wide'), 'tensor'), parts along dimension 0, may hold values from -6 to 6
- fresh_token_value: bfloat16 [128, 1024], P(('rep', 'wide'), 'tensor'), parts along dimension 0, may hold values from -6 to 6
Outputs:
- attention_out: bfloat16 [128, 8192], P(('rep', 'wide')), parts along dimension 0
The draws below stay inside these ranges and needn't reach their ends.
There are 2 independent parts, one for each index of `rep`. The reference program is written for one: setup_inputs(seed, part) draws one part's arguments, and reference() takes and returns one part's arrays. A program takes and returns all parts, laid end to end along the dimension named above; an argument that names none is the same for every part. Nothing has to cross between parts.
Inputs may be any that keep to these rules, and one draw needn't show every extreme that they name: `row_adapter_index`: adapter of each row; a few adapters serve many rows. `adapter_storage_slot`: each adapter's storage slot, each slot used once; slot s lies on index s // 6 of wide.
All inputs are finite; a program needn't handle non-finite values.
Results may differ from the reference program's by a relative error of at most 0.012.
The reference program's roundings to bfloat16 on the way count: a program that leaves them out, or rounds other values in their place, can miss the bound.
Values may be sent and summed in bfloat16 or wider, within the bound.
No kernel may reach another device: no remote copies, remote signals or barrier semaphores. Data moves between devices by JAX's collectives and lax.ppermute only.
A program may use at most 128 MiB of HBM per device.

```python
import math
import jax
import jax.numpy as jnp
import numpy as np
from jax import lax

MODEL_WIDTH = 8192
QUERY_HEADS = 64
KVH = 8
HEAD_SIZE = 128
ADAPTER_RANK = 32
QBLOCK = 64
CACHE = 64
ROWS = 64
ADAPTER_COUNT = 48
GROUP = 8


def draw_stored_key_cache(key, part):
    key = jax.random.fold_in(key, 11)
    base_key = jax.random.fold_in(key, 0)
    array_shape = (ROWS, CACHE, KVH * HEAD_SIZE)
    keys = jax.random.truncated_normal(base_key, -6.0, 6.0, array_shape, jnp.float32)
    return keys.astype(jnp.bfloat16)


def with_ends(entries, rng, least, high):
    longest = entries.shape.index(max(entries.shape))
    spots = []
    for shift in (0, 1):
        where = [jax.random.randint(jax.random.fold_in(rng, axis), (), 0, length) for axis, length in enumerate(entries.shape)]
        where[longest] = (where[longest] + shift) % entries.shape[longest]
        spots.append(tuple(where))
    return entries.at[spots[0]].set(least).at[spots[1]].set(high)


def block_scale(key, extent, shards, low, top_value):
    level, own = 1.0, jax.random.fold_in(key, 6)
    for dim, parts in shards:
        steps = jnp.exp(jax.random.uniform(jax.random.fold_in(own, dim), (parts,), jnp.float32, low / len(shards), top_value / len(shards)))
        level = level * jnp.repeat(steps, extent[dim] // parts).reshape([-1 if axis == dim else 1 for axis in range(len(extent))])
    return level


def rank_bounds(count, lean):
    weights = [(1 << 20) // math.isqrt(rank ** lean) + 1 for rank in range(1, count + 1)]
    scale = 1 + sum(weights) // (1 << 30)
    return np.cumsum(np.array([max(1, weight // scale) for weight in weights]))


def ranked_ids(stream_key, extent, amount, lean):
    grid = rank_bounds(amount, lean)
    ticket = jax.random.randint(jax.random.fold_in(stream_key, 1), extent, 0, int(grid[amount - 1]))
    rank = jnp.searchsorted(jnp.asarray(grid, jnp.int32), ticket, side="right")
    return jax.random.permutation(jax.random.fold_in(stream_key, 2), amount)[rank].astype(jnp.int32)


def noise(rng, shape, spread, bound, pieces=(), dtype=jnp.bfloat16):
    gain = block_scale(rng, shape, pieces, -0.22, 0.18) if pieces else 1.0
    values = jax.random.normal(rng, shape, jnp.float32) * spread * gain
    return jnp.minimum(jnp.maximum(values, -bound), bound).astype(dtype)


def setup_inputs(seed: int = 0, part: int = 0) -> dict:
    key_list = jax.random.split(jax.random.key(seed), 15)
    part_keys = jax.random.split(jax.random.fold_in(key_list[14], part), 15)
    return {
        "tokens": noise(part_keys[0], (ROWS, MODEL_WIDTH), 1.0, 6.0, ((0, 8),)),
        "query_quant_codes": with_ends(jax.random.randint(key_list[1], (MODEL_WIDTH, QUERY_HEADS * HEAD_SIZE), 0, 16), jax.random.fold_in(key_list[1], 1), 0, 15).astype(jnp.int32),
        "query_absmax_scale": jnp.clip(jnp.exp(math.log(0.039774757) - 1.1856236 * jax.random.uniform(key_list[2], (MODEL_WIDTH // QBLOCK, QUERY_HEADS * HEAD_SIZE), jnp.float32) ** block_scale(key_list[2], (MODEL_WIDTH // QBLOCK, QUERY_HEADS * HEAD_SIZE), ((1, 16),), -0.2, 0.2)), 0.012153398, 0.039774757),
        "output_quant_codes": with_ends(jax.random.randint(key_list[3], (QUERY_HEADS * HEAD_SIZE, MODEL_WIDTH), 0, 16), jax.random.fold_in(key_list[3], 1), 0, 15).astype(jnp.int32),
        "output_absmax_scale": jnp.clip(jnp.exp(math.log(0.13258252) - 1.3862944 * jax.random.uniform(key_list[4], (QUERY_HEADS * HEAD_SIZE // QBLOCK, MODEL_WIDTH), jnp.float32) ** block_scale(key_list[4], (QUERY_HEADS * HEAD_SIZE // QBLOCK, MODEL_WIDTH), ((0, 2), (1, 8)), -0.2, 0.2)), 0.03314563, 0.13258252),
        "adapter_down_maps": noise(key_list[5], (MODEL_WIDTH, ADAPTER_COUNT, ADAPTER_RANK), MODEL_WIDTH ** -0.5, 0.0625, ((1, 8),)),
        "adapter_up_maps": noise(key_list[6], (ADAPTER_COUNT, ADAPTER_RANK, QUERY_HEADS * HEAD_SIZE), ADAPTER_RANK ** -0.5, 1.0, ((0, 8), (2, 2))),
        "row_adapter_index": with_ends(ranked_ids(part_keys[7], (ROWS,), ADAPTER_COUNT, 2), jax.random.fold_in(part_keys[7], 3), 0, ADAPTER_COUNT - 1).astype(jnp.int32),
        "adapter_storage_slot": jax.random.permutation(key_list[8], ADAPTER_COUNT).astype(jnp.int32),
        "row_cache_length": with_ends(jax.random.randint(part_keys[9], (ROWS,), 2, CACHE + 1), jax.random.fold_in(part_keys[9], 1), 2, CACHE).astype(jnp.int32),
        "stored_key_cache": draw_stored_key_cache(jax.random.fold_in(jax.random.fold_in(key_list[14], part), 71), part),
        "stored_value_cache": noise(part_keys[11], (ROWS, CACHE, KVH * HEAD_SIZE), 1.0, 6.0, ((0, 8), (2, 2))),
        "fresh_token_key": noise(part_keys[12], (ROWS, KVH * HEAD_SIZE), 1.0, 6.0, ((0, 8), (1, 2))),
        "fresh_token_value": noise(part_keys[13], (ROWS, KVH * HEAD_SIZE), 1.0, 6.0, ((0, 8), (1, 2))),
    }


NF4_LEVELS = (-1.0, -0.6961928009986877, -0.5250730514526367, -0.39491748809814453, -0.28444138169288635, -0.18477343022823334, -0.09105003625154495, 0.0, 0.07958029955625534, 0.16093020141124725, 0.24611230194568634, 0.33791524171829224, 0.44070982933044434, 0.5626170039176941, 0.7229568362236023, 1.0)
ADAPTER_SCALE = 0.5
NEG_LARGE = -1e+30

def dequantize(codes, scales):
    table = jnp.array(NF4_LEVELS, jnp.float32)
    levels = jnp.take(table, codes, axis=0)
    rows, cols = codes.shape
    blocks = levels.reshape(rows // QBLOCK, QBLOCK, cols) * scales[:, None, :]
    return blocks.reshape(rows, cols).astype(jnp.bfloat16)

def reference(tokens, query_quant_codes, query_absmax_scale, output_quant_codes, output_absmax_scale, adapter_down_maps, adapter_up_maps, row_adapter_index, adapter_storage_slot, row_cache_length, stored_key_cache, stored_value_cache, fresh_token_key, fresh_token_value):
    query_weight = dequantize(query_quant_codes, query_absmax_scale)
    output_weight = dequantize(output_quant_codes, output_absmax_scale)
    query_base = jnp.dot(tokens, query_weight, preferred_element_type=jnp.float32).astype(jnp.bfloat16)
    slots = jnp.take(adapter_storage_slot, row_adapter_index, axis=0).astype(jnp.int32)

    def adapt(pair):
        row, storage_position = pair
        down_matrix = lax.dynamic_index_in_dim(adapter_down_maps, storage_position, 1, keepdims=False)
        down_row = jnp.dot(row[None, :], down_matrix, preferred_element_type=jnp.float32).astype(jnp.bfloat16)
        up_matrix = lax.dynamic_index_in_dim(adapter_up_maps, storage_position, 0, keepdims=False)
        return jnp.dot(down_row, up_matrix, preferred_element_type=jnp.float32).astype(jnp.bfloat16)[0]
    adapter_update = lax.map(adapt, (tokens, slots))
    base_query_full = lax.optimization_barrier(query_base).astype(jnp.float32)
    adapter_update_full = lax.optimization_barrier(adapter_update).astype(jnp.float32)
    query_vector = (base_query_full + ADAPTER_SCALE * adapter_update_full).astype(jnp.bfloat16)
    grouped = query_vector.reshape(ROWS, KVH, GROUP, HEAD_SIZE).astype(jnp.float32)
    keys = stored_key_cache.reshape(ROWS, CACHE, KVH, HEAD_SIZE).astype(jnp.float32)
    values = stored_value_cache.reshape(ROWS, CACHE, KVH, HEAD_SIZE).astype(jnp.float32)
    scores = jnp.einsum('rgkd,rtgd->rgkt', grouped, keys) / math.sqrt(HEAD_SIZE)
    valid = jnp.arange(CACHE)[None, :] < row_cache_length[:, None]
    scores = jnp.where(valid[:, None, None, :], scores, NEG_LARGE)
    fresh = jnp.einsum('rgkd,rgd->rgk', grouped, fresh_token_key.reshape(ROWS, KVH, HEAD_SIZE).astype(jnp.float32)) / math.sqrt(HEAD_SIZE)
    highest = jnp.maximum(lax.optimization_barrier(jnp.max(scores, axis=-1)), fresh)
    weights = jnp.exp(scores - highest[..., None])
    fresh_weight = jnp.exp(fresh - highest)
    total = lax.optimization_barrier(jnp.sum(weights, axis=-1)) + fresh_weight
    probs = (weights / total[..., None]).astype(jnp.bfloat16)
    fresh_prob = (fresh_weight / total).astype(jnp.bfloat16)
    context = jnp.einsum('rgkt,rtgd->rgkd', probs.astype(jnp.float32), values)
    context = context + fresh_prob.astype(jnp.float32)[..., None] * fresh_token_value.reshape(ROWS, KVH, 1, HEAD_SIZE).astype(jnp.float32)
    context = context.astype(jnp.bfloat16).reshape(ROWS, QUERY_HEADS * HEAD_SIZE)
    return jnp.dot(context, output_weight, preferred_element_type=jnp.float32).astype(jnp.bfloat16)
```

```python
import math

import jax
import jax.numpy as jnp
import numpy as np
from jax import lax
from jax.experimental import pallas as pl
from jax.experimental.pallas import tpu as pltpu
from jax.sharding import PartitionSpec as P

HEAD_SIZE = 128
QBLOCK = 64
LANES = 128


NF4_LEVELS = (
    -1.0,
    -0.6961928009986877,
    -0.5250730514526367,
    -0.39491748809814453,
    -0.28444138169288635,
    -0.18477343022823334,
    -0.09105003625154495,
    0.0,
    0.07958029955625534,
    0.16093020141124725,
    0.24611230194568634,
    0.33791524171829224,
    0.44070982933044434,
    0.5626170039176941,
    0.7229568362236023,
    1.0,
)
ADAPTER_SCALE = 0.5
NEG_LARGE = -1e30
MIB = 1 << 20
VMEM = pl.BlockSpec(memory_space=pltpu.VMEM)
SMEM = pl.BlockSpec(memory_space=pltpu.SMEM)
ANY = pl.BlockSpec(memory_space=pl.ANY)
LOOKUP = lax.GatherDimensionNumbers(
    offset_dims=(),
    collapsed_slice_dims=(0,),
    start_index_map=(0,),
    operand_batching_dims=(1,),
    start_indices_batching_dims=(1,),
)


def dequantize(codes, scales):
    levels = jnp.zeros(codes.shape, jnp.float32)
    for number, level in enumerate(NF4_LEVELS):
        levels = jnp.where(codes == number, level, levels)
    height, breadth = codes.shape
    blocks = levels.reshape(height // QBLOCK, QBLOCK, breadth) * scales[:, None, :]
    return blocks.reshape(height, breadth).astype(jnp.bfloat16)


def dequantize_part(codes, scales, row, column, height, breadth, after=()):
    chunk = 512
    steps = height // chunk
    blocks = chunk // QBLOCK
    levels = np.repeat(np.array(NF4_LEVELS, np.float32)[:, None], LANES, axis=1)

    def kernel(start, codes_ref, scales_ref, levels_ref, *rest):
        out_ref, held, arrived = rest[-3:]

        def fetch(step):
            return pltpu.make_async_copy(
                codes_ref.at[
                    pl.ds(pl.multiple_of(start[0] + step * chunk, chunk), chunk),
                    pl.ds(pl.multiple_of(start[1], LANES), breadth),
                ],
                held.at[pl.ds(pl.multiple_of(step * chunk, chunk), chunk)],
                arrived.at[step],
            )

        for step in range(steps):
            fetch(step).start()
        table = levels_ref[...]

        def work(step, carry):
            fetch(step).wait()
            first = pl.multiple_of(start[0] // QBLOCK + step * blocks, blocks)
            for lane in range(0, breadth, LANES):
                group = scales_ref[
                    pl.ds(first, blocks), pl.ds(pl.multiple_of(start[1] + lane, LANES), LANES)
                ]
                for block in range(blocks):
                    products = (table * group[block : block + 1]).astype(jnp.bfloat16)
                    at = pl.multiple_of(step * chunk + block * QBLOCK, QBLOCK)
                    numbers = held[pl.ds(at, QBLOCK), lane : lane + LANES].astype(jnp.int16)
                    for piece in range(0, QBLOCK, 16):
                        out_ref[pl.ds(at + piece, 16), lane : lane + LANES] = lax.gather(
                            products,
                            numbers[piece : piece + 16][..., None],
                            LOOKUP,
                            (1, 1),
                            mode=lax.GatherScatterMode.PROMISE_IN_BOUNDS,
                        )
            return carry

        lax.fori_loop(0, steps, work, 0)

    start = jnp.stack([row, column]).astype(jnp.int32)
    return pl.pallas_call(
        kernel,
        in_specs=[SMEM, ANY, VMEM, VMEM] + [ANY] * len(after),
        out_specs=VMEM,
        out_shape=pltpu.VMEM((height, breadth), jnp.bfloat16),
        scratch_shapes=[
            pltpu.VMEM((height, breadth), jnp.int32),
            pltpu.SemaphoreType.DMA((steps,)),
        ],
        compiler_params=pltpu.CompilerParams(vmem_limit_bytes=20 * MIB),
        cost_estimate=pl.CostEstimate(
            flops=2 * height * breadth, bytes_accessed=6 * height * breadth, transcendentals=0
        ),
        name="dequantize",
    )(start, codes, scales, jnp.asarray(levels), *after)


def project_rows(
    place, other_order, own, other, weight_own, weight_other, down, keep_rank, up
):
    count = own[0].shape[0] * 2
    half = own[0].shape[1]
    query_width = weight_own.shape[1]
    ranks, width = up.shape
    block = 8
    chunk = 512

    def kernel(
        place_ref,
        order_ref,
        own_low,
        own_high,
        other_low,
        other_high,
        weight_own_ref,
        weight_other_ref,
        down_ref,
        keep_ref,
        up_ref,
        stay_ref,
        leave_ref,
        query_part,
        down_part,
    ):
        core = place_ref[1]
        mine = jnp.concatenate([own_low[...], own_high[...]], axis=0)
        theirs = jnp.concatenate([other_low[...], other_high[...]], axis=0)
        last = (((1,), (1,)), ((), ()))
        down_part[...] = lax.dot_general(
            theirs,
            down_ref[:, pl.ds(pl.multiple_of((1 - core) * half, half), half)],
            last,
            preferred_element_type=jnp.float32,
        )
        query_part[...] = jnp.dot(
            theirs, weight_other_ref[...], preferred_element_type=jnp.float32
        )
        down_mine = lax.dot_general(
            mine,
            down_ref[:, pl.ds(pl.multiple_of(core * half, half), half)],
            last,
            preferred_element_type=jnp.float32,
        )
        query_mine = jnp.dot(mine, weight_own_ref[...], preferred_element_type=jnp.float32)
        down_rows, query_rows = [], []
        for at in range(0, count, block):
            there = pl.ds(pl.multiple_of(order_ref[at // block] * block, block), block)
            down_rows.append(down_mine[at : at + block] + down_part[there, :])
            query_rows.append(query_mine[at : at + block] + query_part[there, :])
        down_all = jnp.concatenate(down_rows, axis=0)
        query_base = jnp.concatenate(query_rows, axis=0).astype(jnp.bfloat16)
        terms = jnp.where(keep_ref[...] != 0, down_all, 0.0).astype(jnp.bfloat16)
        for lane in range(0, width, chunk):
            delta = jnp.dot(
                terms, up_ref[:, lane : lane + chunk], preferred_element_type=jnp.float32
            ).astype(jnp.bfloat16)
            scaled = (ADAPTER_SCALE * delta.astype(jnp.float32)).astype(jnp.bfloat16)
            stay_ref[:, lane : lane + chunk] = scaled[: count // 2]
            leave_ref[:, lane : lane + chunk] = scaled[count // 2 :]
        here = pl.ds(pl.multiple_of(place_ref[0] * query_width, query_width), query_width)
        base = query_base.astype(jnp.float32)
        stay_ref[:, here] = (base[: count // 2] + stay_ref[:, here].astype(jnp.float32)).astype(
            jnp.bfloat16
        )
        leave_ref[:, here] = (base[count // 2 :] + leave_ref[:, here].astype(jnp.float32)).astype(
            jnp.bfloat16
        )

    shape = jax.ShapeDtypeStruct((count // 2, width), jnp.bfloat16)
    return pl.pallas_call(
        kernel,
        in_specs=[SMEM, SMEM] + [VMEM] * 9,
        out_specs=[VMEM, VMEM],
        out_shape=[shape, shape],
        scratch_shapes=[
            pltpu.VMEM((count, query_width), jnp.float32),
            pltpu.VMEM((count, ranks), jnp.float32),
        ],
        compiler_params=pltpu.CompilerParams(vmem_limit_bytes=24 * MIB),
        cost_estimate=pl.CostEstimate(
            flops=2 * count * (2 * half * (query_width + ranks) + ranks * width),
            bytes_accessed=14 * MIB,
            transcendentals=0,
        ),
        name="project_rows",
    )(place, other_order, *own, *other, weight_own, weight_other, down, keep_rank, up)


def project_out(low, high, weight):
    count = low.shape[0] * 2

    def kernel(low_ref, high_ref, weight_ref, out_ref):
        rows = jnp.concatenate([low_ref[...], high_ref[...]], axis=0)
        out_ref[...] = jnp.dot(rows, weight_ref[...], preferred_element_type=jnp.float32)

    return pl.pallas_call(
        kernel,
        in_specs=[VMEM] * 3,
        out_specs=VMEM,
        out_shape=jax.ShapeDtypeStruct((count, weight.shape[1]), jnp.float32),
        compiler_params=pltpu.CompilerParams(vmem_limit_bytes=12 * MIB),
        cost_estimate=pl.CostEstimate(
            flops=2 * count * weight.shape[0] * weight.shape[1],
            bytes_accessed=6 * MIB,
            transcendentals=0,
        ),
        name="project_out",
    )(low, high, weight)


def sum_halves(targets, other_order, mine, theirs):
    block = 8
    count, width = mine.shape

    def kernel(targets_ref, order_ref, mine_ref, theirs_ref, out_ref):
        for at in range(0, count, block):
            there = pl.ds(pl.multiple_of(order_ref[at // block] * block, block), block)
            out_ref[targets_ref[at // block]] = (
                mine_ref[at : at + block] + theirs_ref[there, :]
            ).astype(jnp.bfloat16)

    return pl.pallas_call(
        kernel,
        in_specs=[SMEM, SMEM, VMEM, VMEM],
        out_specs=VMEM,
        out_shape=jax.ShapeDtypeStruct((count // block, block, width), jnp.bfloat16),
        name="sum_halves",
    )(targets, other_order, mine, theirs)


def join_columns(place, mine, theirs):
    sources, rows, width = mine.shape

    def kernel(place_ref, mine_ref, theirs_ref, out_ref):
        core = place_ref[1]
        for source in range(sources):
            first = source * 2 * width
            out_ref[:, pl.ds(pl.multiple_of(first + core * width, width), width)] = mine_ref[source]
            out_ref[:, pl.ds(pl.multiple_of(first + (1 - core) * width, width), width)] = (
                theirs_ref[source]
            )

    return pl.pallas_call(
        kernel,
        in_specs=[SMEM, VMEM, VMEM],
        out_specs=VMEM,
        out_shape=jax.ShapeDtypeStruct((rows, sources * 2 * width), mine.dtype),
        name="join_columns",
    )(place, mine, theirs)


def attend(
    query_vector,
    row_cache_length,
    stored_key_cache,
    stored_value_cache,
    fresh_token_key,
    fresh_token_value,
):
    rows_dev = query_vector.shape[0]
    kv_local = stored_key_cache.shape[2] // HEAD_SIZE
    length = stored_key_cache.shape[1]
    grouped = query_vector.reshape(rows_dev, kv_local, -1, HEAD_SIZE)
    keys = stored_key_cache.reshape(rows_dev, length, kv_local, HEAD_SIZE)
    values = stored_value_cache.reshape(rows_dev, length, kv_local, HEAD_SIZE)
    scores = jnp.einsum(
        "rgkd,rtgd->rgkt", grouped, keys, preferred_element_type=jnp.float32
    ) / math.sqrt(HEAD_SIZE)
    valid = jnp.arange(length)[None, :] < row_cache_length[:, None]
    scores = jnp.where(valid[:, None, None, :], scores, NEG_LARGE)
    fresh = jnp.einsum(
        "rgkd,rgd->rgk",
        grouped,
        fresh_token_key.reshape(rows_dev, kv_local, HEAD_SIZE),
        preferred_element_type=jnp.float32,
    ) / math.sqrt(HEAD_SIZE)
    highest = jnp.maximum(jnp.max(scores, axis=-1), fresh)
    weights = jnp.exp(scores - highest[..., None])
    fresh_weight = jnp.exp(fresh - highest)
    total = jnp.sum(weights, axis=-1) + fresh_weight
    probs = (weights / total[..., None]).astype(jnp.bfloat16)
    fresh_prob = (fresh_weight / total).astype(jnp.bfloat16)
    context = jnp.einsum("rgkt,rtgd->rgkd", probs, values, preferred_element_type=jnp.float32)
    context = context + fresh_prob.astype(jnp.float32)[..., None] * fresh_token_value.reshape(
        rows_dev, kv_local, 1, HEAD_SIZE
    ).astype(jnp.float32)
    return context.astype(jnp.bfloat16).reshape(
        rows_dev, kv_local * grouped.shape[2] * HEAD_SIZE
    )


def plain(
    tokens,
    query_quant_codes,
    query_absmax_scale,
    output_quant_codes,
    output_absmax_scale,
    adapter_down_maps,
    adapter_up_maps,
    row_adapter_index,
    adapter_storage_slot,
    row_cache_length,
    stored_key_cache,
    stored_value_cache,
    fresh_token_key,
    fresh_token_value,
):
    query_weight = dequantize(query_quant_codes, query_absmax_scale)
    query_width = query_weight.shape[1]
    owned_portion = adapter_down_maps.shape[1]
    adapter_rank_size = adapter_down_maps.shape[2]
    down_matrix_flat = adapter_down_maps.reshape(
        adapter_down_maps.shape[0], owned_portion * adapter_rank_size
    )
    joined = jnp.concatenate([query_weight, down_matrix_flat], axis=1)
    projected = jnp.dot(
        lax.all_gather(tokens, "wide", axis=0, tiled=True),
        joined,
        preferred_element_type=jnp.float32,
    )
    query_base = projected[:, :query_width].astype(jnp.bfloat16)
    down_all = projected[:, query_width:]
    matches = row_adapter_index[:, None] == jnp.arange(adapter_storage_slot.shape[0])[None, :]
    slots = jnp.sum(jnp.where(matches, adapter_storage_slot[None, :], 0), axis=1)
    local_slot = slots - lax.axis_index("wide") * owned_portion
    query_transferred = lax.all_to_all(query_base, "wide", split_axis=0, concat_axis=1, tiled=True)
    column_owner = jnp.arange(owned_portion * adapter_rank_size) // adapter_rank_size
    keep = column_owner[None, :] == local_slot[:, None]
    rank_terms = jnp.where(keep, down_all, 0.0).astype(jnp.bfloat16)
    up_matrix_flat = adapter_up_maps.reshape(
        owned_portion * adapter_rank_size, adapter_up_maps.shape[2]
    )
    rounded = jnp.dot(rank_terms, up_matrix_flat, preferred_element_type=jnp.float32).astype(
        jnp.bfloat16
    )
    adapter_update = lax.psum_scatter(
        lax.optimization_barrier(rounded).astype(jnp.float32),
        "wide",
        scatter_dimension=0,
        tiled=True,
    )
    query_vector = (query_transferred.astype(jnp.float32) + ADAPTER_SCALE * adapter_update).astype(
        jnp.bfloat16
    )
    context = attend(
        query_vector,
        row_cache_length,
        stored_key_cache,
        stored_value_cache,
        fresh_token_key,
        fresh_token_value,
    )
    output_weight = dequantize(output_quant_codes, output_absmax_scale)
    partial_out = jnp.dot(
        lax.all_gather(context, "wide", axis=0, tiled=True),
        output_weight,
        preferred_element_type=jnp.float32,
    )
    summed = lax.psum(partial_out, "tensor")
    routed = lax.all_to_all(
        summed.astype(jnp.bfloat16), "wide", split_axis=0, concat_axis=1, tiled=True
    )
    return routed


def fast(
    wide,
    tokens,
    query_quant_codes,
    query_absmax_scale,
    output_quant_codes,
    output_absmax_scale,
    adapter_down_maps,
    adapter_up_maps,
    row_adapter_index,
    adapter_storage_slot,
    row_cache_length,
    stored_key_cache,
    stored_value_cache,
    fresh_token_key,
    fresh_token_value,
):
    rows_dev, model_width = tokens.shape
    half = model_width // 2
    rounds = wide.bit_length() - 1
    flips = [list(range(rounds))[::-1], [0] + list(range(1, rounds))[::-1]]
    offsets = np.zeros((2, wide), np.int32)
    for core in range(2):
        for number in range(rounds):
            for at in range(wide):
                offsets[core, at] |= ((at >> number) & 1) << flips[core][number]
    positions = np.argsort(offsets, axis=1)
    orders = np.stack([positions[1 - core][offsets[core]] for core in range(2)]).astype(np.int32)

    me = lax.axis_index("wide").astype(jnp.int32)
    core = lax.axis_index("tensor").astype(jnp.int32)
    place = jnp.stack([me, core])
    first_core = core == 0
    other_order = jnp.where(first_core, orders[0], orders[1])
    targets = me ^ jnp.where(first_core, offsets[0], offsets[1])

    def swap(array, number):
        pairs = [
            (peer * 2 + side, (peer ^ (1 << flips[side][number])) * 2 + side)
            for peer in range(wide)
            for side in range(2)
        ]
        return lax.ppermute(array, ("wide", "tensor"), pairs)

    def cross(array):
        return lax.ppermute(array, "tensor", [(0, 1), (1, 0)])

    def gather_rows(array):
        for number in range(rounds - 1):
            array = jnp.concatenate([array, swap(array, number)], axis=0)
        return array, swap(array, rounds - 1)

    own = gather_rows(lax.dynamic_slice(tokens, (0, core * half), (rows_dev, half)))
    other = [cross(part) for part in own]

    weight_own = dequantize_part(
        query_quant_codes,
        query_absmax_scale,
        core * half,
        jnp.int32(0),
        half,
        query_quant_codes.shape[1],
    )
    weight_other = dequantize_part(
        query_quant_codes,
        query_absmax_scale,
        (1 - core) * half,
        jnp.int32(0),
        half,
        query_quant_codes.shape[1],
    )
    out_height, out_width = output_quant_codes.shape
    out_half = out_width // 2
    out_leave = dequantize_part(
        output_quant_codes,
        output_absmax_scale,
        jnp.int32(0),
        (1 - core) * out_half,
        out_height,
        out_half,
    )
    out_stay = dequantize_part(
        output_quant_codes,
        output_absmax_scale,
        jnp.int32(0),
        core * out_half,
        out_height,
        out_half,
    )

    owned, rank = adapter_down_maps.shape[1:]
    all_rows = (targets[:, None] * rows_dev + jnp.arange(rows_dev)[None, :]).reshape(-1)
    picked = all_rows[:, None] == jnp.arange(all_rows.shape[0])[None, :]
    adapters = jnp.sum(jnp.where(picked, row_adapter_index[None, :], 0), axis=1)
    matches = adapters[:, None] == jnp.arange(adapter_storage_slot.shape[0])[None, :]
    slots = jnp.sum(jnp.where(matches, adapter_storage_slot[None, :], 0), axis=1)
    rank_owner = jnp.arange(owned * rank) // rank + me * owned
    keep_rank = (rank_owner[None, :] == slots[:, None]).astype(jnp.int32)

    down = adapter_down_maps.transpose(1, 2, 0).reshape(owned * rank, model_width)
    up = adapter_up_maps.reshape(owned * rank, adapter_up_maps.shape[2])
    stay, leave = project_rows(
        place, other_order, own, other, weight_own, weight_other, down, keep_rank, up
    )

    for number in range(rounds)[::-1]:
        total = stay + swap(leave, number)
        keep = total.shape[0] // 2
        stay, leave = total[:keep], total[keep:]
    query_vector = total

    context = attend(
        query_vector,
        row_cache_length,
        stored_key_cache,
        stored_value_cache,
        fresh_token_key,
        fresh_token_value,
    )
    low, high = gather_rows(context)
    theirs = cross(project_out(low, high, out_leave))
    mine = project_out(low, high, out_stay)
    routed = lax.all_to_all(sum_halves(targets, other_order, mine, theirs), "wide", 0, 0)
    return join_columns(place, routed, cross(routed))


def solution(mesh):
    in_specs = (
        P(("rep", "wide"), None),
        P(None, ("tensor", "wide")),
        P(None, ("tensor", "wide")),
        P("tensor", "wide"),
        P("tensor", "wide"),
        P(None, "wide", None),
        P("wide", None, "tensor"),
        P("rep"),
        P(),
        P(("rep", "wide")),
        P(("rep", "wide"), None, "tensor"),
        P(("rep", "wide"), None, "tensor"),
        P(("rep", "wide"), "tensor"),
        P(("rep", "wide"), "tensor"),
    )
    out_specs = P(("rep", "wide"), None)
    wide = mesh.shape["wide"]

    def on_device(*args):
        query_width, out_width = args[1].shape[1], args[3].shape[1]
        whole_tiles = query_width % LANES == 0 and out_width % (2 * LANES) == 0
        return fast(wide, *args) if whole_tiles else plain(*args)

    return jax.shard_map(
        on_device, mesh=mesh, in_specs=in_specs, out_specs=out_specs, check_vma=False
    )
```

```python
import math

import jax
import jax.numpy as jnp
import numpy as np
from jax import lax
from jax.experimental import pallas as pl
from jax.experimental.pallas import tpu as pltpu
from jax.sharding import PartitionSpec as P

HEAD_SIZE = 128
QBLOCK = 64
LANES = 128


NF4_LEVELS = (
    -1.0,
    -0.6961928009986877,
    -0.5250730514526367,
    -0.39491748809814453,
    -0.28444138169288635,
    -0.18477343022823334,
    -0.09105003625154495,
    0.0,
    0.07958029955625534,
    0.16093020141124725,
    0.24611230194568634,
    0.33791524171829224,
    0.44070982933044434,
    0.5626170039176941,
    0.7229568362236023,
    1.0,
)
ADAPTER_SCALE = 0.5
NEG_LARGE = -1e30
MIB = 1 << 20
VMEM = pl.BlockSpec(memory_space=pltpu.VMEM)
SMEM = pl.BlockSpec(memory_space=pltpu.SMEM)
ANY = pl.BlockSpec(memory_space=pl.ANY)
LOOKUP = lax.GatherDimensionNumbers(
    offset_dims=(),
    collapsed_slice_dims=(0,),
    start_index_map=(0,),
    operand_batching_dims=(1,),
    start_indices_batching_dims=(1,),
)


def dequantize(codes, scales):
    levels = jnp.zeros(codes.shape, jnp.float32)
    for number, level in enumerate(NF4_LEVELS):
        levels = jnp.where(codes == number, level, levels)
    height, breadth = codes.shape
    blocks = levels.reshape(height // QBLOCK, QBLOCK, breadth) * scales[:, None, :]
    return blocks.reshape(height, breadth).astype(jnp.bfloat16)


def dequantize_part(codes, scales, segments, column, breadth, room, sent):
    chunk = 512
    height = sum(rows for _, rows in segments)
    steps = height // chunk
    blocks = chunk // QBLOCK
    starts = [first + at for first, rows in segments for at in range(0, rows, chunk)]
    starts, _ = lax.optimization_barrier((jnp.stack([column] + starts).astype(jnp.int32), sent))

    def kernel(starts_ref, codes_ref, scales_ref, out_ref, held, factors, arrived, factors_arrived):
        columns = pl.ds(pl.multiple_of(starts_ref[0], LANES), breadth)

        def fetch(step):
            return pltpu.make_async_copy(
                codes_ref.at[pl.ds(pl.multiple_of(starts_ref[step + 1], chunk), chunk), columns],
                held.at[pl.ds(pl.multiple_of(step * chunk, chunk), chunk)],
                arrived.at[step],
            )

        def fetch_factors(step):
            first = pl.multiple_of(starts_ref[step + 1] // QBLOCK, blocks)
            return pltpu.make_async_copy(
                scales_ref.at[pl.ds(first, blocks), columns],
                factors.at[pl.ds(pl.multiple_of(step * blocks, blocks), blocks)],
                factors_arrived.at[step],
            )

        for step in range(steps):
            fetch_factors(step).start()
            fetch(step).start()
        number = lax.broadcasted_iota(jnp.int32, (16, LANES), 0)
        table = jnp.zeros((16, LANES), jnp.float32)
        for code, level in enumerate(NF4_LEVELS):
            table = jnp.where(number == code, level, table)

        def work(step, carry):
            fetch_factors(step).wait()
            fetch(step).wait()
            for lane in range(0, breadth, LANES):
                group = factors[
                    pl.ds(pl.multiple_of(step * blocks, blocks), blocks), lane : lane + LANES
                ]
                for block in range(blocks):
                    products = (table * group[block : block + 1]).astype(jnp.bfloat16)
                    at = pl.multiple_of(step * chunk + block * QBLOCK, QBLOCK)
                    numbers = held[pl.ds(at, QBLOCK), lane : lane + LANES].astype(jnp.int16)
                    for piece in range(0, QBLOCK, 16):
                        out_ref[pl.ds(at + piece, 16), lane : lane + LANES] = lax.gather(
                            products,
                            numbers[piece : piece + 16][..., None],
                            LOOKUP,
                            (1, 1),
                            mode=lax.GatherScatterMode.PROMISE_IN_BOUNDS,
                        )
            return carry

        lax.fori_loop(0, steps, work, 0)

    return pl.pallas_call(
        kernel,
        in_specs=[SMEM, ANY, ANY],
        out_specs=VMEM,
        out_shape=pltpu.VMEM((height, breadth), jnp.bfloat16),
        scratch_shapes=[
            pltpu.VMEM((height, breadth), jnp.int32),
            pltpu.VMEM((height // QBLOCK, breadth), jnp.float32),
            pltpu.SemaphoreType.DMA((steps,)),
            pltpu.SemaphoreType.DMA((steps,)),
        ],
        compiler_params=pltpu.CompilerParams(vmem_limit_bytes=room * MIB),
        cost_estimate=pl.CostEstimate(
            flops=2 * height * breadth, bytes_accessed=6 * height * breadth, transcendentals=0
        ),
        name="dequantize",
    )(starts, codes, scales)


LAST = (((1,), (1,)), ((), ()))


def project_own(place, own, first_weight, rest_weight, down):
    count = own[0].shape[0] * 2
    half = own[0].shape[1]
    cut, query_width = first_weight.shape

    def kernel(place_ref, low, high, first_ref, rest_ref, down_ref, query_ref, rank_ref):
        rows = jnp.concatenate([low[...], high[...]], axis=0)
        here = pl.ds(pl.multiple_of(place_ref[1] * half, half), half)
        rank_ref[...] = lax.dot_general(
            rows, down_ref[:, here], LAST, preferred_element_type=jnp.float32
        )
        query_ref[...] = jnp.dot(
            rows[:, :cut], first_ref[...], preferred_element_type=jnp.float32
        ) + jnp.dot(rows[:, cut:], rest_ref[: half - cut], preferred_element_type=jnp.float32)

    return pl.pallas_call(
        kernel,
        in_specs=[SMEM] + [VMEM] * 5,
        out_specs=[VMEM, VMEM],
        out_shape=[
            jax.ShapeDtypeStruct((count, query_width), jnp.float32),
            jax.ShapeDtypeStruct((count, down.shape[0]), jnp.float32),
        ],
        compiler_params=pltpu.CompilerParams(vmem_limit_bytes=24 * MIB),
        cost_estimate=pl.CostEstimate(
            flops=2 * count * half * (query_width + down.shape[0]),
            bytes_accessed=7 * MIB,
            transcendentals=0,
        ),
        name="project_own",
    )(place, *own, first_weight, rest_weight, down)


def project_other(place, other, rest_weight, down, query_mine, rank_mine, keep_rank, up):
    count = other[0].shape[0] * 2
    half = other[0].shape[1]
    query_width = rest_weight.shape[1]
    width = up.shape[1]
    chunk = 512

    def kernel(
        place_ref,
        low,
        high,
        rest_ref,
        down_ref,
        query_ref,
        rank_ref,
        keep_ref,
        up_ref,
        stay_ref,
        leave_ref,
    ):
        rows = jnp.concatenate([low[...], high[...]], axis=0)
        there = pl.ds(pl.multiple_of((1 - place_ref[1]) * half, half), half)
        ranks = rank_ref[...] + lax.dot_general(
            rows, down_ref[:, there], LAST, preferred_element_type=jnp.float32
        )
        terms = jnp.where(keep_ref[...] != 0, ranks, 0.0).astype(jnp.bfloat16)
        query = query_ref[...] + jnp.dot(
            rows, rest_ref[rest_ref.shape[0] - half :], preferred_element_type=jnp.float32
        )
        base = query.astype(jnp.bfloat16).astype(jnp.float32)
        for lane in range(0, width, chunk):
            delta = jnp.dot(
                terms, up_ref[:, lane : lane + chunk], preferred_element_type=jnp.float32
            ).astype(jnp.bfloat16)
            scaled = (ADAPTER_SCALE * delta.astype(jnp.float32)).astype(jnp.bfloat16)
            stay_ref[:, lane : lane + chunk] = scaled[: count // 2]
            leave_ref[:, lane : lane + chunk] = scaled[count // 2 :]
        here = pl.ds(pl.multiple_of(place_ref[0] * query_width, query_width), query_width)
        stay_ref[:, here] = (base[: count // 2] + stay_ref[:, here].astype(jnp.float32)).astype(
            jnp.bfloat16
        )
        leave_ref[:, here] = (base[count // 2 :] + leave_ref[:, here].astype(jnp.float32)).astype(
            jnp.bfloat16
        )

    shape = jax.ShapeDtypeStruct((count // 2, width), jnp.bfloat16)
    return pl.pallas_call(
        kernel,
        in_specs=[SMEM] + [VMEM] * 8,
        out_specs=[VMEM, VMEM],
        out_shape=[shape, shape],
        compiler_params=pltpu.CompilerParams(vmem_limit_bytes=24 * MIB),
        cost_estimate=pl.CostEstimate(
            flops=2 * count * (half * (query_width + up.shape[0]) + up.shape[0] * width),
            bytes_accessed=8 * MIB,
            transcendentals=0,
        ),
        name="project_other",
    )(place, *other, rest_weight, down, query_mine, rank_mine, keep_rank, up)


def project_out(low, high, weight):
    count = low.shape[0] * 2

    def kernel(low_ref, high_ref, weight_ref, out_ref):
        rows = jnp.concatenate([low_ref[...], high_ref[...]], axis=0)
        out_ref[...] = jnp.dot(rows, weight_ref[...], preferred_element_type=jnp.float32)

    return pl.pallas_call(
        kernel,
        in_specs=[VMEM] * 3,
        out_specs=VMEM,
        out_shape=jax.ShapeDtypeStruct((count, weight.shape[1]), jnp.float32),
        compiler_params=pltpu.CompilerParams(vmem_limit_bytes=12 * MIB),
        cost_estimate=pl.CostEstimate(
            flops=2 * count * weight.shape[0] * weight.shape[1],
            bytes_accessed=6 * MIB,
            transcendentals=0,
        ),
        name="project_out",
    )(low, high, weight)


def sum_halves(targets, mine, theirs):
    block = 8
    count, width = mine.shape

    def kernel(targets_ref, mine_ref, theirs_ref, out_ref):
        for at in range(0, count, block):
            rows = (mine_ref[at : at + block] + theirs_ref[at : at + block]).astype(jnp.bfloat16)
            for side in range(2):
                out_ref[targets_ref[at // block] * 2 + side] = rows

    return pl.pallas_call(
        kernel,
        in_specs=[SMEM, VMEM, VMEM],
        out_specs=VMEM,
        out_shape=jax.ShapeDtypeStruct((count // block * 2, block, width), jnp.bfloat16),
        compiler_params=pltpu.CompilerParams(vmem_limit_bytes=4 * MIB),
        name="sum_halves",
    )(targets, mine, theirs)


def join_columns(pieces):
    sources, rows, width = pieces.shape

    def kernel(pieces_ref, out_ref):
        for source in range(sources):
            out_ref[:, source * width : (source + 1) * width] = pieces_ref[source]

    return pl.pallas_call(
        kernel,
        in_specs=[VMEM],
        out_specs=VMEM,
        out_shape=jax.ShapeDtypeStruct((rows, sources * width), pieces.dtype),
        compiler_params=pltpu.CompilerParams(vmem_limit_bytes=4 * MIB),
        name="join_columns",
    )(pieces)


def attend(
    query_vector,
    row_cache_length,
    stored_key_cache,
    stored_value_cache,
    fresh_token_key,
    fresh_token_value,
):
    rows_dev = query_vector.shape[0]
    kv_local = stored_key_cache.shape[2] // HEAD_SIZE
    length = stored_key_cache.shape[1]
    grouped = query_vector.reshape(rows_dev, kv_local, -1, HEAD_SIZE)
    keys = stored_key_cache.reshape(rows_dev, length, kv_local, HEAD_SIZE)
    values = stored_value_cache.reshape(rows_dev, length, kv_local, HEAD_SIZE)
    scores = jnp.einsum(
        "rgkd,rtgd->rgkt", grouped, keys, preferred_element_type=jnp.float32
    ) / math.sqrt(HEAD_SIZE)
    valid = jnp.arange(length)[None, :] < row_cache_length[:, None]
    scores = jnp.where(valid[:, None, None, :], scores, NEG_LARGE)
    fresh = jnp.einsum(
        "rgkd,rgd->rgk",
        grouped,
        fresh_token_key.reshape(rows_dev, kv_local, HEAD_SIZE),
        preferred_element_type=jnp.float32,
    ) / math.sqrt(HEAD_SIZE)
    highest = jnp.maximum(jnp.max(scores, axis=-1), fresh)
    weights = jnp.exp(scores - highest[..., None])
    fresh_weight = jnp.exp(fresh - highest)
    total = jnp.sum(weights, axis=-1) + fresh_weight
    probs = (weights / total[..., None]).astype(jnp.bfloat16)
    fresh_prob = (fresh_weight / total).astype(jnp.bfloat16)
    context = jnp.einsum("rgkt,rtgd->rgkd", probs, values, preferred_element_type=jnp.float32)
    context = context + fresh_prob.astype(jnp.float32)[..., None] * fresh_token_value.reshape(
        rows_dev, kv_local, 1, HEAD_SIZE
    ).astype(jnp.float32)
    return context.astype(jnp.bfloat16).reshape(
        rows_dev, kv_local * grouped.shape[2] * HEAD_SIZE
    )


def plain(
    tokens,
    query_quant_codes,
    query_absmax_scale,
    output_quant_codes,
    output_absmax_scale,
    adapter_down_maps,
    adapter_up_maps,
    row_adapter_index,
    adapter_storage_slot,
    row_cache_length,
    stored_key_cache,
    stored_value_cache,
    fresh_token_key,
    fresh_token_value,
):
    query_weight = dequantize(query_quant_codes, query_absmax_scale)
    query_width = query_weight.shape[1]
    owned_portion = adapter_down_maps.shape[1]
    adapter_rank_size = adapter_down_maps.shape[2]
    down_matrix_flat = adapter_down_maps.reshape(
        adapter_down_maps.shape[0], owned_portion * adapter_rank_size
    )
    joined = jnp.concatenate([query_weight, down_matrix_flat], axis=1)
    projected = jnp.dot(
        lax.all_gather(tokens, "wide", axis=0, tiled=True),
        joined,
        preferred_element_type=jnp.float32,
    )
    query_base = projected[:, :query_width].astype(jnp.bfloat16)
    down_all = projected[:, query_width:]
    matches = row_adapter_index[:, None] == jnp.arange(adapter_storage_slot.shape[0])[None, :]
    slots = jnp.sum(jnp.where(matches, adapter_storage_slot[None, :], 0), axis=1)
    local_slot = slots - lax.axis_index("wide") * owned_portion
    query_transferred = lax.all_to_all(query_base, "wide", split_axis=0, concat_axis=1, tiled=True)
    column_owner = jnp.arange(owned_portion * adapter_rank_size) // adapter_rank_size
    keep = column_owner[None, :] == local_slot[:, None]
    rank_terms = jnp.where(keep, down_all, 0.0).astype(jnp.bfloat16)
    up_matrix_flat = adapter_up_maps.reshape(
        owned_portion * adapter_rank_size, adapter_up_maps.shape[2]
    )
    rounded = jnp.dot(rank_terms, up_matrix_flat, preferred_element_type=jnp.float32).astype(
        jnp.bfloat16
    )
    adapter_update = lax.psum_scatter(
        lax.optimization_barrier(rounded).astype(jnp.float32),
        "wide",
        scatter_dimension=0,
        tiled=True,
    )
    query_vector = (query_transferred.astype(jnp.float32) + ADAPTER_SCALE * adapter_update).astype(
        jnp.bfloat16
    )
    context = attend(
        query_vector,
        row_cache_length,
        stored_key_cache,
        stored_value_cache,
        fresh_token_key,
        fresh_token_value,
    )
    output_weight = dequantize(output_quant_codes, output_absmax_scale)
    partial_out = jnp.dot(
        lax.all_gather(context, "wide", axis=0, tiled=True),
        output_weight,
        preferred_element_type=jnp.float32,
    )
    summed = lax.psum(partial_out, "tensor")
    routed = lax.all_to_all(
        summed.astype(jnp.bfloat16), "wide", split_axis=0, concat_axis=1, tiled=True
    )
    return routed


def fast(
    wide,
    tokens,
    query_quant_codes,
    query_absmax_scale,
    output_quant_codes,
    output_absmax_scale,
    adapter_down_maps,
    adapter_up_maps,
    row_adapter_index,
    adapter_storage_slot,
    row_cache_length,
    stored_key_cache,
    stored_value_cache,
    fresh_token_key,
    fresh_token_value,
):
    rows_dev, model_width = tokens.shape
    half = model_width // 2
    rounds = wide.bit_length() - 1
    offsets = np.zeros(wide, np.int32)
    for number in range(rounds):
        for at in range(wide):
            offsets[at] |= ((at >> number) & 1) << (rounds - 1 - number)

    me = lax.axis_index("wide").astype(jnp.int32)
    core = lax.axis_index("tensor").astype(jnp.int32)
    zero = jnp.int32(0)
    place = jnp.stack([me, core])
    targets = me ^ offsets

    def swap(array, number):
        bit = 1 << (rounds - 1 - number)
        return lax.ppermute(array, "wide", [(peer, peer ^ bit) for peer in range(wide)])

    def cross(array):
        return lax.ppermute(array, "tensor", [(0, 1), (1, 0)])

    def beside(work, sent, received):
        if work is None:
            return received, None
        return lax.optimization_barrier((received, work(sent)))

    def gather_rows(array, works):
        made = []
        for number in range(rounds):
            work = works.get(rounds - 1 - number)
            received, result = beside(work, array, swap(array, number))
            made.append(result)
            if number < rounds - 1:
                array = jnp.concatenate([array, received], axis=0)
        return (array, received), made[::-1]

    query_width = query_quant_codes.shape[1]
    out_height, out_width = output_quant_codes.shape
    out_half = out_width // 2
    cut = half // 2
    own_row, other_row = core * half, (1 - core) * half

    def query_first(sent):
        return dequantize_part(
            query_quant_codes,
            query_absmax_scale,
            [(own_row, cut)],
            zero,
            query_width,
            50,
            sent,
        )

    def query_rest(sent):
        return dequantize_part(
            query_quant_codes,
            query_absmax_scale,
            [(own_row + cut, half - cut), (other_row, half)],
            zero,
            query_width,
            46,
            sent,
        )

    def out_part(column):
        return lambda sent: dequantize_part(
            output_quant_codes,
            output_absmax_scale,
            [(zero, out_height)],
            column,
            out_half,
            47,
            sent,
        )

    own, made = gather_rows(
        lax.dynamic_slice(tokens, (0, core * half), (rows_dev, half)),
        {1: query_first, 0: query_rest},
    )
    rest_weight, first_weight = made[:2]
    other = [cross(part) for part in own]

    owned, rank = adapter_down_maps.shape[1:]
    all_rows = (targets[:, None] * rows_dev + jnp.arange(rows_dev)[None, :]).reshape(-1)
    picked = all_rows[:, None] == jnp.arange(all_rows.shape[0])[None, :]
    adapters = jnp.sum(jnp.where(picked, row_adapter_index[None, :], 0), axis=1)
    matches = adapters[:, None] == jnp.arange(adapter_storage_slot.shape[0])[None, :]
    slots = jnp.sum(jnp.where(matches, adapter_storage_slot[None, :], 0), axis=1)
    rank_owner = jnp.arange(owned * rank) // rank + me * owned
    keep_rank = (rank_owner[None, :] == slots[:, None]).astype(jnp.int32)

    down = adapter_down_maps.transpose(1, 2, 0).reshape(owned * rank, model_width)
    up = adapter_up_maps.reshape(owned * rank, adapter_up_maps.shape[2])
    query_mine, rank_mine = project_own(place, own, first_weight, rest_weight, down)
    stay, leave = project_other(
        place, other, rest_weight, down, query_mine, rank_mine, keep_rank, up
    )

    out_leave = None
    for number in range(rounds)[::-1]:
        work = out_part((1 - core) * out_half) if number == rounds - 1 else None
        received, result = beside(work, leave, swap(leave, number))
        out_leave = out_leave if result is None else result
        total = stay + received
        keep = total.shape[0] // 2
        stay, leave = total[:keep], total[keep:]

    context = attend(
        total,
        row_cache_length,
        stored_key_cache,
        stored_value_cache,
        fresh_token_key,
        fresh_token_value,
    )
    (low, high), made = gather_rows(context, {0: out_part(core * out_half)})
    out_stay = made[0]
    theirs = cross(project_out(low, high, out_leave))
    mine = project_out(low, high, out_stay)
    routed = lax.all_to_all(sum_halves(targets, mine, theirs), ("wide", "tensor"), 0, 0)
    return join_columns(routed)


def solution(mesh):
    in_specs = (
        P(("rep", "wide"), None),
        P(None, ("tensor", "wide")),
        P(None, ("tensor", "wide")),
        P("tensor", "wide"),
        P("tensor", "wide"),
        P(None, "wide", None),
        P("wide", None, "tensor"),
        P("rep"),
        P(),
        P(("rep", "wide")),
        P(("rep", "wide"), None, "tensor"),
        P(("rep", "wide"), None, "tensor"),
        P(("rep", "wide"), "tensor"),
        P(("rep", "wide"), "tensor"),
    )
    out_specs = P(("rep", "wide"), None)
    wide = mesh.shape["wide"]

    def on_device(*args):
        query_width, out_width = args[1].shape[1], args[3].shape[1]
        whole_tiles = query_width % LANES == 0 and out_width % (2 * LANES) == 0
        return fast(wide, *args) if whole_tiles else plain(*args)

    return jax.shard_map(
        on_device, mesh=mesh, in_specs=in_specs, out_specs=out_specs, check_vma=False
    )
```

```python
import math

import jax
import jax.numpy as jnp
import numpy as np
from jax import lax
from jax.experimental import pallas as pl
from jax.experimental.pallas import tpu as pltpu
from jax.sharding import PartitionSpec as P

HEAD_SIZE = 128
QBLOCK = 64
LANES = 128


NF4_LEVELS = (
    -1.0,
    -0.6961928009986877,
    -0.5250730514526367,
    -0.39491748809814453,
    -0.28444138169288635,
    -0.18477343022823334,
    -0.09105003625154495,
    0.0,
    0.07958029955625534,
    0.16093020141124725,
    0.24611230194568634,
    0.33791524171829224,
    0.44070982933044434,
    0.5626170039176941,
    0.7229568362236023,
    1.0,
)
ADAPTER_SCALE = 0.5
NEG_LARGE = -1e30
MIB = 1 << 20
VMEM = pl.BlockSpec(memory_space=pltpu.VMEM)
SMEM = pl.BlockSpec(memory_space=pltpu.SMEM)
ANY = pl.BlockSpec(memory_space=pl.ANY)
LOOKUP = lax.GatherDimensionNumbers(
    offset_dims=(),
    collapsed_slice_dims=(0,),
    start_index_map=(0,),
    operand_batching_dims=(1,),
    start_indices_batching_dims=(1,),
)


def dequantize(codes, scales):
    levels = jnp.zeros(codes.shape, jnp.float32)
    for number, level in enumerate(NF4_LEVELS):
        levels = jnp.where(codes == number, level, levels)
    height, breadth = codes.shape
    blocks = levels.reshape(height // QBLOCK, QBLOCK, breadth) * scales[:, None, :]
    return blocks.reshape(height, breadth).astype(jnp.bfloat16)


def dequantize_part(codes, scales, segments, column, breadth, room, sent):
    chunk = 512
    height = sum(rows for _, rows in segments)
    steps = height // chunk
    blocks = chunk // QBLOCK
    starts = [first + at for first, rows in segments for at in range(0, rows, chunk)]
    starts, _ = lax.optimization_barrier((jnp.stack([column] + starts).astype(jnp.int32), sent))

    def kernel(starts_ref, codes_ref, scales_ref, out_ref, held, factors, arrived, factors_arrived):
        columns = pl.ds(pl.multiple_of(starts_ref[0], LANES), breadth)

        def fetch(step):
            return pltpu.make_async_copy(
                codes_ref.at[pl.ds(pl.multiple_of(starts_ref[step + 1], chunk), chunk), columns],
                held.at[pl.ds(pl.multiple_of(step * chunk, chunk), chunk)],
                arrived.at[step],
            )

        def fetch_factors(step):
            first = pl.multiple_of(starts_ref[step + 1] // QBLOCK, blocks)
            return pltpu.make_async_copy(
                scales_ref.at[pl.ds(first, blocks), columns],
                factors.at[pl.ds(pl.multiple_of(step * blocks, blocks), blocks)],
                factors_arrived.at[step],
            )

        for step in range(steps):
            fetch_factors(step).start()
            fetch(step).start()
        number = lax.broadcasted_iota(jnp.int32, (16, LANES), 0)
        table = jnp.zeros((16, LANES), jnp.float32)
        for code, level in enumerate(NF4_LEVELS):
            table = jnp.where(number == code, level, table)

        def work(step, carry):
            fetch_factors(step).wait()
            fetch(step).wait()
            for lane in range(0, breadth, LANES):
                group = factors[
                    pl.ds(pl.multiple_of(step * blocks, blocks), blocks), lane : lane + LANES
                ]
                for block in range(blocks):
                    products = (table * group[block : block + 1]).astype(jnp.bfloat16)
                    at = pl.multiple_of(step * chunk + block * QBLOCK, QBLOCK)
                    numbers = held[pl.ds(at, QBLOCK), lane : lane + LANES].astype(jnp.int16)
                    for piece in range(0, QBLOCK, 16):
                        out_ref[pl.ds(at + piece, 16), lane : lane + LANES] = lax.gather(
                            products,
                            numbers[piece : piece + 16][..., None],
                            LOOKUP,
                            (1, 1),
                            mode=lax.GatherScatterMode.PROMISE_IN_BOUNDS,
                        )
            return carry

        lax.fori_loop(0, steps, work, 0)

    return pl.pallas_call(
        kernel,
        in_specs=[SMEM, ANY, ANY],
        out_specs=VMEM,
        out_shape=pltpu.VMEM((height, breadth), jnp.bfloat16),
        scratch_shapes=[
            pltpu.VMEM((height, breadth), jnp.int32),
            pltpu.VMEM((height // QBLOCK, breadth), jnp.float32),
            pltpu.SemaphoreType.DMA((steps,)),
            pltpu.SemaphoreType.DMA((steps,)),
        ],
        compiler_params=pltpu.CompilerParams(vmem_limit_bytes=room * MIB),
        cost_estimate=pl.CostEstimate(
            flops=2 * height * breadth, bytes_accessed=6 * height * breadth, transcendentals=0
        ),
        name="dequantize",
    )(starts, codes, scales)


LAST = (((1,), (1,)), ((), ()))


def project_own(place, own, weight, down):
    count = own[0].shape[0] * 2
    half = own[0].shape[1]
    query_width = weight.shape[1]

    def kernel(place_ref, low, high, weight_ref, down_ref, query_ref, rank_ref):
        rows = jnp.concatenate([low[...], high[...]], axis=0)
        here = pl.ds(pl.multiple_of(place_ref[1] * half, half), half)
        rank_ref[...] = lax.dot_general(
            down_ref[:, here], rows, LAST, preferred_element_type=jnp.float32
        )
        query_ref[...] = jnp.dot(rows, weight_ref[...], preferred_element_type=jnp.float32)

    return pl.pallas_call(
        kernel,
        in_specs=[SMEM] + [VMEM] * 4,
        out_specs=[VMEM, VMEM],
        out_shape=[
            jax.ShapeDtypeStruct((count, query_width), jnp.float32),
            jax.ShapeDtypeStruct((down.shape[0], count), jnp.float32),
        ],
        compiler_params=pltpu.CompilerParams(vmem_limit_bytes=24 * MIB),
        cost_estimate=pl.CostEstimate(
            flops=2 * count * half * (query_width + down.shape[0]),
            bytes_accessed=7 * MIB,
            transcendentals=0,
        ),
        name="project_own",
    )(place, *own, weight, down)


def project_other(place, other, weight, down, query_mine, rank_mine, keep_rank, up):
    count = other[0].shape[0] * 2
    half = other[0].shape[1]
    query_width = weight.shape[1]
    width = up.shape[1]
    chunk = 512

    def kernel(
        place_ref,
        low,
        high,
        weight_ref,
        down_ref,
        query_ref,
        rank_ref,
        keep_ref,
        up_ref,
        stay_ref,
        leave_ref,
    ):
        rows = jnp.concatenate([low[...], high[...]], axis=0)
        there = pl.ds(pl.multiple_of((1 - place_ref[1]) * half, half), half)
        ranks = rank_ref[...] + lax.dot_general(
            down_ref[:, there], rows, LAST, preferred_element_type=jnp.float32
        )
        terms = jnp.where(keep_ref[...] != 0, ranks.T, 0.0).astype(jnp.bfloat16)
        query = query_ref[...] + jnp.dot(
            rows, weight_ref[...], preferred_element_type=jnp.float32
        )
        base = query.astype(jnp.bfloat16).astype(jnp.float32)
        for lane in range(0, width, chunk):
            delta = jnp.dot(
                terms, up_ref[:, lane : lane + chunk], preferred_element_type=jnp.float32
            ).astype(jnp.bfloat16)
            scaled = (ADAPTER_SCALE * delta.astype(jnp.float32)).astype(jnp.bfloat16)
            stay_ref[:, lane : lane + chunk] = scaled[: count // 2]
            leave_ref[:, lane : lane + chunk] = scaled[count // 2 :]
        here = pl.ds(pl.multiple_of(place_ref[0] * query_width, query_width), query_width)
        stay_ref[:, here] = (base[: count // 2] + stay_ref[:, here].astype(jnp.float32)).astype(
            jnp.bfloat16
        )
        leave_ref[:, here] = (base[count // 2 :] + leave_ref[:, here].astype(jnp.float32)).astype(
            jnp.bfloat16
        )

    shape = jax.ShapeDtypeStruct((count // 2, width), jnp.bfloat16)
    return pl.pallas_call(
        kernel,
        in_specs=[SMEM] + [VMEM] * 8,
        out_specs=[VMEM, VMEM],
        out_shape=[shape, shape],
        compiler_params=pltpu.CompilerParams(vmem_limit_bytes=24 * MIB),
        cost_estimate=pl.CostEstimate(
            flops=2 * count * (half * (query_width + up.shape[0]) + up.shape[0] * width),
            bytes_accessed=8 * MIB,
            transcendentals=0,
        ),
        name="project_other",
    )(place, *other, weight, down, query_mine, rank_mine, keep_rank, up)


def project_out(low, high, weight):
    count = low.shape[0] * 2

    def kernel(low_ref, high_ref, weight_ref, out_ref):
        rows = jnp.concatenate([low_ref[...], high_ref[...]], axis=0)
        out_ref[...] = jnp.dot(rows, weight_ref[...], preferred_element_type=jnp.float32)

    return pl.pallas_call(
        kernel,
        in_specs=[VMEM] * 3,
        out_specs=VMEM,
        out_shape=jax.ShapeDtypeStruct((count, weight.shape[1]), jnp.float32),
        compiler_params=pltpu.CompilerParams(vmem_limit_bytes=12 * MIB),
        cost_estimate=pl.CostEstimate(
            flops=2 * count * weight.shape[0] * weight.shape[1],
            bytes_accessed=6 * MIB,
            transcendentals=0,
        ),
        name="project_out",
    )(low, high, weight)


def sum_halves(targets, mine, theirs):
    block = 8
    count, width = mine.shape

    def kernel(targets_ref, mine_ref, theirs_ref, out_ref):
        for at in range(0, count, block):
            rows = (mine_ref[at : at + block] + theirs_ref[at : at + block]).astype(jnp.bfloat16)
            for side in range(2):
                out_ref[targets_ref[at // block] * 2 + side] = rows

    return pl.pallas_call(
        kernel,
        in_specs=[SMEM, VMEM, VMEM],
        out_specs=VMEM,
        out_shape=jax.ShapeDtypeStruct((count // block * 2, block, width), jnp.bfloat16),
        compiler_params=pltpu.CompilerParams(vmem_limit_bytes=4 * MIB),
        name="sum_halves",
    )(targets, mine, theirs)


def join_columns(pieces):
    sources, rows, width = pieces.shape

    def kernel(pieces_ref, out_ref):
        for source in range(sources):
            out_ref[:, source * width : (source + 1) * width] = pieces_ref[source]

    return pl.pallas_call(
        kernel,
        in_specs=[VMEM],
        out_specs=VMEM,
        out_shape=jax.ShapeDtypeStruct((rows, sources * width), pieces.dtype),
        compiler_params=pltpu.CompilerParams(vmem_limit_bytes=4 * MIB),
        name="join_columns",
    )(pieces)


def attend(
    query_vector,
    row_cache_length,
    stored_key_cache,
    stored_value_cache,
    fresh_token_key,
    fresh_token_value,
):
    rows_dev = query_vector.shape[0]
    kv_local = stored_key_cache.shape[2] // HEAD_SIZE
    length = stored_key_cache.shape[1]
    grouped = query_vector.reshape(rows_dev, kv_local, -1, HEAD_SIZE)
    keys = stored_key_cache.reshape(rows_dev, length, kv_local, HEAD_SIZE)
    values = stored_value_cache.reshape(rows_dev, length, kv_local, HEAD_SIZE)
    scores = jnp.einsum(
        "rgkd,rtgd->rgkt", grouped, keys, preferred_element_type=jnp.float32
    ) / math.sqrt(HEAD_SIZE)
    valid = jnp.arange(length)[None, :] < row_cache_length[:, None]
    scores = jnp.where(valid[:, None, None, :], scores, NEG_LARGE)
    fresh = jnp.einsum(
        "rgkd,rgd->rgk",
        grouped,
        fresh_token_key.reshape(rows_dev, kv_local, HEAD_SIZE),
        preferred_element_type=jnp.float32,
    ) / math.sqrt(HEAD_SIZE)
    highest = jnp.maximum(jnp.max(scores, axis=-1), fresh)
    weights = jnp.exp(scores - highest[..., None])
    fresh_weight = jnp.exp(fresh - highest)
    total = jnp.sum(weights, axis=-1) + fresh_weight
    probs = (weights / total[..., None]).astype(jnp.bfloat16)
    fresh_prob = (fresh_weight / total).astype(jnp.bfloat16)
    context = jnp.einsum("rgkt,rtgd->rgkd", probs, values, preferred_element_type=jnp.float32)
    context = context + fresh_prob.astype(jnp.float32)[..., None] * fresh_token_value.reshape(
        rows_dev, kv_local, 1, HEAD_SIZE
    ).astype(jnp.float32)
    return context.astype(jnp.bfloat16).reshape(
        rows_dev, kv_local * grouped.shape[2] * HEAD_SIZE
    )


def plain(
    tokens,
    query_quant_codes,
    query_absmax_scale,
    output_quant_codes,
    output_absmax_scale,
    adapter_down_maps,
    adapter_up_maps,
    row_adapter_index,
    adapter_storage_slot,
    row_cache_length,
    stored_key_cache,
    stored_value_cache,
    fresh_token_key,
    fresh_token_value,
):
    query_weight = dequantize(query_quant_codes, query_absmax_scale)
    query_width = query_weight.shape[1]
    owned_portion = adapter_down_maps.shape[1]
    adapter_rank_size = adapter_down_maps.shape[2]
    down_matrix_flat = adapter_down_maps.reshape(
        adapter_down_maps.shape[0], owned_portion * adapter_rank_size
    )
    joined = jnp.concatenate([query_weight, down_matrix_flat], axis=1)
    projected = jnp.dot(
        lax.all_gather(tokens, "wide", axis=0, tiled=True),
        joined,
        preferred_element_type=jnp.float32,
    )
    query_base = projected[:, :query_width].astype(jnp.bfloat16)
    down_all = projected[:, query_width:]
    matches = row_adapter_index[:, None] == jnp.arange(adapter_storage_slot.shape[0])[None, :]
    slots = jnp.sum(jnp.where(matches, adapter_storage_slot[None, :], 0), axis=1)
    local_slot = slots - lax.axis_index("wide") * owned_portion
    query_transferred = lax.all_to_all(query_base, "wide", split_axis=0, concat_axis=1, tiled=True)
    column_owner = jnp.arange(owned_portion * adapter_rank_size) // adapter_rank_size
    keep = column_owner[None, :] == local_slot[:, None]
    rank_terms = jnp.where(keep, down_all, 0.0).astype(jnp.bfloat16)
    up_matrix_flat = adapter_up_maps.reshape(
        owned_portion * adapter_rank_size, adapter_up_maps.shape[2]
    )
    rounded = jnp.dot(rank_terms, up_matrix_flat, preferred_element_type=jnp.float32).astype(
        jnp.bfloat16
    )
    adapter_update = lax.psum_scatter(
        lax.optimization_barrier(rounded).astype(jnp.float32),
        "wide",
        scatter_dimension=0,
        tiled=True,
    )
    query_vector = (query_transferred.astype(jnp.float32) + ADAPTER_SCALE * adapter_update).astype(
        jnp.bfloat16
    )
    context = attend(
        query_vector,
        row_cache_length,
        stored_key_cache,
        stored_value_cache,
        fresh_token_key,
        fresh_token_value,
    )
    output_weight = dequantize(output_quant_codes, output_absmax_scale)
    partial_out = jnp.dot(
        lax.all_gather(context, "wide", axis=0, tiled=True),
        output_weight,
        preferred_element_type=jnp.float32,
    )
    summed = lax.psum(partial_out, "tensor")
    routed = lax.all_to_all(
        summed.astype(jnp.bfloat16), "wide", split_axis=0, concat_axis=1, tiled=True
    )
    return routed


def fast(
    wide,
    tokens,
    query_quant_codes,
    query_absmax_scale,
    output_quant_codes,
    output_absmax_scale,
    adapter_down_maps,
    adapter_up_maps,
    row_adapter_index,
    adapter_storage_slot,
    row_cache_length,
    stored_key_cache,
    stored_value_cache,
    fresh_token_key,
    fresh_token_value,
):
    rows_dev, model_width = tokens.shape
    half = model_width // 2
    offsets = np.array([far * 2 + near for near in range(2) for far in range(wide // 2)], np.int32)

    me = lax.axis_index("wide").astype(jnp.int32)
    core = lax.axis_index("tensor").astype(jnp.int32)
    zero = jnp.int32(0)
    place = jnp.stack([me, core])
    targets = me ^ offsets

    def swap(array, offset):
        return lax.ppermute(array, "wide", [(peer, peer ^ offset) for peer in range(wide)])

    def cross(array):
        return lax.ppermute(array, "tensor", [(0, 1), (1, 0)])

    def beside(work, sent, received):
        return lax.optimization_barrier((received, work(sent)))

    far_offsets = range(2, wide, 2)

    query_width = query_quant_codes.shape[1]
    out_height, out_width = output_quant_codes.shape
    out_half = out_width // 2

    def query_part(row, room):
        return lambda sent: dequantize_part(
            query_quant_codes, query_absmax_scale, [(row, half)], zero, query_width, room, sent
        )

    def out_part(column, room):
        return lambda sent: dequantize_part(
            output_quant_codes,
            output_absmax_scale,
            [(zero, out_height)],
            column,
            out_half,
            room,
            sent,
        )

    block = lax.dynamic_slice(tokens, (0, core * half), (rows_dev, half))
    arrived, weight_own = beside(
        query_part(core * half, 50), block, [swap(block, offset) for offset in far_offsets]
    )
    low = jnp.concatenate([block] + arrived, axis=0)
    high, weight_other = beside(query_part((1 - core) * half, 48), low, swap(low, 1))
    own = (low, high)
    other = [cross(part) for part in own]

    owned, rank = adapter_down_maps.shape[1:]
    all_rows = (targets[:, None] * rows_dev + jnp.arange(rows_dev)[None, :]).reshape(-1)
    picked = all_rows[:, None] == jnp.arange(all_rows.shape[0])[None, :]
    adapters = jnp.sum(jnp.where(picked, row_adapter_index[None, :], 0), axis=1)
    matches = adapters[:, None] == jnp.arange(adapter_storage_slot.shape[0])[None, :]
    slots = jnp.sum(jnp.where(matches, adapter_storage_slot[None, :], 0), axis=1)
    rank_owner = jnp.arange(owned * rank) // rank + me * owned
    keep_rank = (rank_owner[None, :] == slots[:, None]).astype(jnp.int32)

    down = adapter_down_maps.transpose(1, 2, 0).reshape(owned * rank, model_width)
    up = adapter_up_maps.reshape(owned * rank, adapter_up_maps.shape[2])
    query_mine, rank_mine = project_own(place, own, weight_own, down)
    stay, leave = project_other(
        place, other, weight_other, down, query_mine, rank_mine, keep_rank, up
    )

    received, out_leave = beside(out_part((1 - core) * out_half, 46), leave, swap(leave, 1))
    stay = stay + received
    blocks = [stay[at : at + rows_dev] for at in range(0, stay.shape[0], rows_dev)]
    arrived, out_stay = beside(
        out_part(core * out_half, 44),
        stay,
        [swap(part, offset) for part, offset in zip(blocks[1:], far_offsets)],
    )
    query_vector = sum(arrived, blocks[0])

    context = attend(
        query_vector,
        row_cache_length,
        stored_key_cache,
        stored_value_cache,
        fresh_token_key,
        fresh_token_value,
    )
    arrived = [context] + [swap(context, offset) for offset in far_offsets]
    low = jnp.concatenate(arrived, axis=0)
    high = jnp.concatenate([swap(part, 1) for part in arrived], axis=0)
    theirs = cross(project_out(low, high, out_leave))
    mine = project_out(low, high, out_stay)
    routed = lax.all_to_all(sum_halves(targets, mine, theirs), ("wide", "tensor"), 0, 0)
    return join_columns(routed)


def solution(mesh):
    in_specs = (
        P(("rep", "wide"), None),
        P(None, ("tensor", "wide")),
        P(None, ("tensor", "wide")),
        P("tensor", "wide"),
        P("tensor", "wide"),
        P(None, "wide", None),
        P("wide", None, "tensor"),
        P("rep"),
        P(),
        P(("rep", "wide")),
        P(("rep", "wide"), None, "tensor"),
        P(("rep", "wide"), None, "tensor"),
        P(("rep", "wide"), "tensor"),
        P(("rep", "wide"), "tensor"),
    )
    out_specs = P(("rep", "wide"), None)
    wide = mesh.shape["wide"]

    def on_device(*args):
        query_width, out_width = args[1].shape[1], args[3].shape[1]
        whole_tiles = query_width % LANES == 0 and out_width % (2 * LANES) == 0
        return fast(wide, *args) if whole_tiles else plain(*args)

    return jax.shard_map(
        on_device, mesh=mesh, in_specs=in_specs, out_specs=out_specs, check_vma=False
    )
```

```python
import math

import jax
import jax.numpy as jnp
import numpy as np
from jax import lax
from jax.experimental import pallas as pl
from jax.experimental.pallas import tpu as pltpu
from jax.sharding import PartitionSpec as P

HEAD_SIZE = 128
QBLOCK = 64
LANES = 128


NF4_LEVELS = (
    -1.0,
    -0.6961928009986877,
    -0.5250730514526367,
    -0.39491748809814453,
    -0.28444138169288635,
    -0.18477343022823334,
    -0.09105003625154495,
    0.0,
    0.07958029955625534,
    0.16093020141124725,
    0.24611230194568634,
    0.33791524171829224,
    0.44070982933044434,
    0.5626170039176941,
    0.7229568362236023,
    1.0,
)
ADAPTER_SCALE = 0.5
NEG_LARGE = -1e30
MIB = 1 << 20
VMEM = pl.BlockSpec(memory_space=pltpu.VMEM)
SMEM = pl.BlockSpec(memory_space=pltpu.SMEM)
ANY = pl.BlockSpec(memory_space=pl.ANY)
LOOKUP = lax.GatherDimensionNumbers(
    offset_dims=(),
    collapsed_slice_dims=(0,),
    start_index_map=(0,),
    operand_batching_dims=(1,),
    start_indices_batching_dims=(1,),
)


def dequantize(codes, scales):
    levels = jnp.zeros(codes.shape, jnp.float32)
    for number, level in enumerate(NF4_LEVELS):
        levels = jnp.where(codes == number, level, levels)
    height, breadth = codes.shape
    blocks = levels.reshape(height // QBLOCK, QBLOCK, breadth) * scales[:, None, :]
    return blocks.reshape(height, breadth).astype(jnp.bfloat16)


def dequantize_all(place, codes, scales, halves):
    chunk = 512
    height, breadth = codes.shape
    blocks = chunk // QBLOCK
    parts = 2 if halves else 1
    width = breadth // parts

    def kernel(place_ref, codes_ref, scales_ref, out_ref):
        number = lax.broadcasted_iota(jnp.int32, (16, LANES), 0)
        table = jnp.zeros((16, LANES), jnp.float32)
        for code, level in enumerate(NF4_LEVELS):
            table = jnp.where(number == code, level, table)

        def work(step, carry):
            for lane in range(0, breadth, LANES):
                part = lane // width
                place_in = (part + 1 + place_ref[1]) % 2 if halves else 0
                group = scales_ref[
                    pl.ds(pl.multiple_of(step * blocks, blocks), blocks), lane : lane + LANES
                ]
                for block in range(blocks):
                    products = (table * group[block : block + 1]).astype(jnp.bfloat16)
                    at = pl.multiple_of(step * chunk + block * QBLOCK, QBLOCK)
                    numbers = codes_ref[pl.ds(at, QBLOCK), lane : lane + LANES].astype(jnp.int16)
                    to = lane - part * width
                    for piece in range(0, QBLOCK, 16):
                        out_ref[place_in, pl.ds(at + piece, 16), to : to + LANES] = lax.gather(
                            products,
                            numbers[piece : piece + 16][..., None],
                            LOOKUP,
                            (1, 1),
                            mode=lax.GatherScatterMode.PROMISE_IN_BOUNDS,
                        )
            return carry

        lax.fori_loop(0, height // chunk, work, 0)

    return pl.pallas_call(
        kernel,
        in_specs=[SMEM, VMEM, VMEM],
        out_specs=VMEM,
        out_shape=pltpu.VMEM((parts, height, width), jnp.bfloat16),
        compiler_params=pltpu.CompilerParams(vmem_limit_bytes=2 * MIB),
        cost_estimate=pl.CostEstimate(
            flops=2 * height * breadth, bytes_accessed=6 * height * breadth, transcendentals=0
        ),
        name="dequantize",
    )(place, codes, scales)


def begin_gather(place, block):
    def kernel(place_ref, block_ref, out_ref):
        out_ref[...] = block_ref[...]

    return pl.pallas_call(
        kernel,
        in_specs=[SMEM, VMEM],
        out_specs=VMEM,
        out_shape=pltpu.VMEM(block.shape, block.dtype),
        compiler_params=pltpu.CompilerParams(vmem_limit_bytes=2 * MIB),
        cost_estimate=pl.CostEstimate(
            flops=6_000_000_000, bytes_accessed=4 * block.size, transcendentals=0
        ),
        name="begin_gather",
    )(place, block)


LAST = (((1,), (1,)), ((), ()))


def project_own(place, offsets, row_adapter_index, adapter_storage_slot, own, weight, down):
    count = own[0].shape[0] * 2
    half = own[0].shape[1]
    query_width = weight.shape[2]
    block = count // len(offsets)

    def kernel(
        place_ref,
        adapters_ref,
        storage_ref,
        low,
        high,
        weight_ref,
        down_ref,
        query_ref,
        rank_ref,
        slots_ref,
    ):
        rows = jnp.concatenate([low[...], high[...]], axis=0)
        here = pl.ds(pl.multiple_of(place_ref[1] * half, half), half)
        rank_ref[...] = lax.dot_general(
            down_ref[:, here], rows, LAST, preferred_element_type=jnp.float32
        )
        query_ref[...] = jnp.dot(rows, weight_ref[0, here], preferred_element_type=jnp.float32)
        column = lax.broadcasted_iota(jnp.int32, slots_ref.shape, 1)
        slots = jnp.zeros(slots_ref.shape, jnp.int32)
        for row in range(count):
            source = (place_ref[0] ^ int(offsets[row // block])) * block + row % block
            slots = jnp.where(column == row, storage_ref[adapters_ref[source]], slots)
        slots_ref[...] = slots

    return pl.pallas_call(
        kernel,
        in_specs=[SMEM] * 3 + [VMEM] * 4,
        out_specs=[VMEM] * 3,
        out_shape=[
            jax.ShapeDtypeStruct((count, query_width), jnp.float32),
            jax.ShapeDtypeStruct((down.shape[0], count), jnp.float32),
            jax.ShapeDtypeStruct((8, count), jnp.int32),
        ],
        compiler_params=pltpu.CompilerParams(vmem_limit_bytes=4 * MIB),
        cost_estimate=pl.CostEstimate(
            flops=2 * count * half * (query_width + down.shape[0]),
            bytes_accessed=7 * MIB,
            transcendentals=0,
        ),
        name="project_own",
    )(place, row_adapter_index, adapter_storage_slot, *own, weight, down)


def project_other(place, other, weight, down, query_mine, rank_mine, slots, owned, up):
    count = other[0].shape[0] * 2
    half = other[0].shape[1]
    query_width = weight.shape[2]
    width = up.shape[1]
    rank = up.shape[0] // owned
    part = count // 4
    chunk = 512

    def kernel(
        place_ref,
        low,
        high,
        weight_ref,
        down_ref,
        query_ref,
        rank_ref,
        slots_ref,
        up_ref,
        *out_refs,
    ):
        rows = jnp.concatenate([low[...], high[...]], axis=0)
        there = pl.ds(pl.multiple_of((1 - place_ref[1]) * half, half), half)
        ranks = rank_ref[...] + lax.dot_general(
            down_ref[:, there], rows, LAST, preferred_element_type=jnp.float32
        )
        slot = slots_ref[:1]
        kept = [
            jnp.where(slot == place_ref[0] * owned + number, ranks[at : at + rank], 0.0)
            for number, at in enumerate(range(0, owned * rank, rank))
        ]
        terms = jnp.concatenate(kept, axis=0).T.astype(jnp.bfloat16)
        query = query_ref[...] + jnp.dot(
            rows, weight_ref[0, there], preferred_element_type=jnp.float32
        )
        base = query.astype(jnp.bfloat16).astype(jnp.float32)
        for lane in range(0, width, chunk):
            delta = jnp.dot(
                terms, up_ref[:, lane : lane + chunk], preferred_element_type=jnp.float32
            ).astype(jnp.bfloat16)
            scaled = (ADAPTER_SCALE * delta.astype(jnp.float32)).astype(jnp.bfloat16)
            for number, out_ref in enumerate(out_refs):
                out_ref[:, lane : lane + chunk] = scaled[number * part : (number + 1) * part]
        here = pl.ds(pl.multiple_of(place_ref[0] * query_width, query_width), query_width)
        for number, out_ref in enumerate(out_refs):
            rows_base = base[number * part : (number + 1) * part]
            out_ref[:, here] = (rows_base + out_ref[:, here].astype(jnp.float32)).astype(
                jnp.bfloat16
            )

    shape = jax.ShapeDtypeStruct((part, width), jnp.bfloat16)
    return pl.pallas_call(
        kernel,
        in_specs=[SMEM] + [VMEM] * 8,
        out_specs=[VMEM] * 4,
        out_shape=[shape] * 4,
        compiler_params=pltpu.CompilerParams(vmem_limit_bytes=4 * MIB),
        cost_estimate=pl.CostEstimate(
            flops=2 * count * (half * (query_width + up.shape[0]) + up.shape[0] * width),
            bytes_accessed=8 * MIB,
            transcendentals=0,
        ),
        name="project_other",
    )(place, *other, weight, down, query_mine, rank_mine, slots, up)


def project_out(low, high, weight, part):
    count = low.shape[0] * 2
    _, height, breadth = weight.shape

    def kernel(low_ref, high_ref, weight_ref, out_ref):
        rows = jnp.concatenate([low_ref[...], high_ref[...]], axis=0)
        out_ref[...] = jnp.dot(rows, weight_ref[part], preferred_element_type=jnp.float32)

    return pl.pallas_call(
        kernel,
        in_specs=[VMEM] * 3,
        out_specs=VMEM,
        out_shape=jax.ShapeDtypeStruct((count, breadth), jnp.float32),
        compiler_params=pltpu.CompilerParams(vmem_limit_bytes=4 * MIB),
        cost_estimate=pl.CostEstimate(
            flops=2 * count * height * breadth, bytes_accessed=6 * MIB, transcendentals=0
        ),
        name="project_out",
    )(low, high, weight)


def sum_halves(place, offsets, mine, theirs):
    block = 8
    count, width = mine.shape

    def kernel(place_ref, mine_ref, theirs_ref, out_ref):
        for number, at in enumerate(range(0, count, block)):
            rows = (mine_ref[at : at + block] + theirs_ref[at : at + block]).astype(jnp.bfloat16)
            for side in range(2):
                out_ref[(place_ref[0] ^ int(offsets[number])) * 2 + side] = rows

    return pl.pallas_call(
        kernel,
        in_specs=[SMEM, VMEM, VMEM],
        out_specs=VMEM,
        out_shape=jax.ShapeDtypeStruct((count // block * 2, block, width), jnp.bfloat16),
        compiler_params=pltpu.CompilerParams(vmem_limit_bytes=4 * MIB),
        name="sum_halves",
    )(place, mine, theirs)


def join_columns(pieces):
    sources, rows, width = pieces.shape

    def kernel(pieces_ref, out_ref):
        for source in range(sources):
            out_ref[:, source * width : (source + 1) * width] = pieces_ref[source]

    return pl.pallas_call(
        kernel,
        in_specs=[VMEM],
        out_specs=VMEM,
        out_shape=jax.ShapeDtypeStruct((rows, sources * width), pieces.dtype),
        compiler_params=pltpu.CompilerParams(vmem_limit_bytes=4 * MIB),
        name="join_columns",
    )(pieces)


def attend(
    query_vector,
    row_cache_length,
    stored_key_cache,
    stored_value_cache,
    fresh_token_key,
    fresh_token_value,
):
    rows_dev = query_vector.shape[0]
    kv_local = stored_key_cache.shape[2] // HEAD_SIZE
    length = stored_key_cache.shape[1]
    grouped = query_vector.reshape(rows_dev, kv_local, -1, HEAD_SIZE)
    keys = stored_key_cache.reshape(rows_dev, length, kv_local, HEAD_SIZE)
    values = stored_value_cache.reshape(rows_dev, length, kv_local, HEAD_SIZE)
    scores = jnp.einsum(
        "rgkd,rtgd->rgkt", grouped, keys, preferred_element_type=jnp.float32
    ) / math.sqrt(HEAD_SIZE)
    valid = jnp.arange(length)[None, :] < row_cache_length[:, None]
    scores = jnp.where(valid[:, None, None, :], scores, NEG_LARGE)
    fresh = jnp.einsum(
        "rgkd,rgd->rgk",
        grouped,
        fresh_token_key.reshape(rows_dev, kv_local, HEAD_SIZE),
        preferred_element_type=jnp.float32,
    ) / math.sqrt(HEAD_SIZE)
    highest = jnp.maximum(jnp.max(scores, axis=-1), fresh)
    weights = jnp.exp(scores - highest[..., None])
    fresh_weight = jnp.exp(fresh - highest)
    total = jnp.sum(weights, axis=-1) + fresh_weight
    probs = (weights / total[..., None]).astype(jnp.bfloat16)
    fresh_prob = (fresh_weight / total).astype(jnp.bfloat16)
    context = jnp.einsum("rgkt,rtgd->rgkd", probs, values, preferred_element_type=jnp.float32)
    context = context + fresh_prob.astype(jnp.float32)[..., None] * fresh_token_value.reshape(
        rows_dev, kv_local, 1, HEAD_SIZE
    ).astype(jnp.float32)
    return context.astype(jnp.bfloat16).reshape(
        rows_dev, kv_local * grouped.shape[2] * HEAD_SIZE
    )


def plain(
    tokens,
    query_quant_codes,
    query_absmax_scale,
    output_quant_codes,
    output_absmax_scale,
    adapter_down_maps,
    adapter_up_maps,
    row_adapter_index,
    adapter_storage_slot,
    row_cache_length,
    stored_key_cache,
    stored_value_cache,
    fresh_token_key,
    fresh_token_value,
):
    query_weight = dequantize(query_quant_codes, query_absmax_scale)
    query_width = query_weight.shape[1]
    owned_portion = adapter_down_maps.shape[1]
    adapter_rank_size = adapter_down_maps.shape[2]
    down_matrix_flat = adapter_down_maps.reshape(
        adapter_down_maps.shape[0], owned_portion * adapter_rank_size
    )
    joined = jnp.concatenate([query_weight, down_matrix_flat], axis=1)
    projected = jnp.dot(
        lax.all_gather(tokens, "wide", axis=0, tiled=True),
        joined,
        preferred_element_type=jnp.float32,
    )
    query_base = projected[:, :query_width].astype(jnp.bfloat16)
    down_all = projected[:, query_width:]
    matches = row_adapter_index[:, None] == jnp.arange(adapter_storage_slot.shape[0])[None, :]
    slots = jnp.sum(jnp.where(matches, adapter_storage_slot[None, :], 0), axis=1)
    local_slot = slots - lax.axis_index("wide") * owned_portion
    query_transferred = lax.all_to_all(query_base, "wide", split_axis=0, concat_axis=1, tiled=True)
    column_owner = jnp.arange(owned_portion * adapter_rank_size) // adapter_rank_size
    keep = column_owner[None, :] == local_slot[:, None]
    rank_terms = jnp.where(keep, down_all, 0.0).astype(jnp.bfloat16)
    up_matrix_flat = adapter_up_maps.reshape(
        owned_portion * adapter_rank_size, adapter_up_maps.shape[2]
    )
    rounded = jnp.dot(rank_terms, up_matrix_flat, preferred_element_type=jnp.float32).astype(
        jnp.bfloat16
    )
    adapter_update = lax.psum_scatter(
        lax.optimization_barrier(rounded).astype(jnp.float32),
        "wide",
        scatter_dimension=0,
        tiled=True,
    )
    query_vector = (query_transferred.astype(jnp.float32) + ADAPTER_SCALE * adapter_update).astype(
        jnp.bfloat16
    )
    context = attend(
        query_vector,
        row_cache_length,
        stored_key_cache,
        stored_value_cache,
        fresh_token_key,
        fresh_token_value,
    )
    output_weight = dequantize(output_quant_codes, output_absmax_scale)
    partial_out = jnp.dot(
        lax.all_gather(context, "wide", axis=0, tiled=True),
        output_weight,
        preferred_element_type=jnp.float32,
    )
    summed = lax.psum(partial_out, "tensor")
    routed = lax.all_to_all(
        summed.astype(jnp.bfloat16), "wide", split_axis=0, concat_axis=1, tiled=True
    )
    return routed


def fast(
    wide,
    tokens,
    query_quant_codes,
    query_absmax_scale,
    output_quant_codes,
    output_absmax_scale,
    adapter_down_maps,
    adapter_up_maps,
    row_adapter_index,
    adapter_storage_slot,
    row_cache_length,
    stored_key_cache,
    stored_value_cache,
    fresh_token_key,
    fresh_token_value,
):
    rows_dev, model_width = tokens.shape
    half = model_width // 2
    offsets = np.array([far * 2 + near for near in range(2) for far in range(wide // 2)], np.int32)

    me = lax.axis_index("wide").astype(jnp.int32)
    core = lax.axis_index("tensor").astype(jnp.int32)
    place = jnp.stack([me, core])

    def swap(array, offset):
        return lax.ppermute(array, "wide", [(peer, peer ^ offset) for peer in range(wide)])

    def cross(array):
        return lax.ppermute(array, "tensor", [(0, 1), (1, 0)])

    far_offsets = range(2, wide, 2)

    block = lax.dynamic_slice(tokens, (0, core * half), (rows_dev, half))
    block = begin_gather(place, block)
    blocks = [block] + [swap(block, offset) for offset in far_offsets]
    query_weight = dequantize_all(place, query_quant_codes, query_absmax_scale, False)
    blocks[1:] = [lax.optimization_barrier((part, query_weight))[0] for part in blocks[1:]]
    low = jnp.concatenate(blocks, axis=0)
    high = jnp.concatenate([swap(part, 1) for part in blocks], axis=0)
    own = (low, high)
    other = [cross(part) for part in own]

    owned, rank = adapter_down_maps.shape[1:]
    down = adapter_down_maps.transpose(1, 2, 0).reshape(owned * rank, model_width)
    up = adapter_up_maps.reshape(owned * rank, adapter_up_maps.shape[2])
    query_mine, rank_mine, slots = project_own(
        place, offsets, row_adapter_index, adapter_storage_slot, own, query_weight, down
    )
    stay_low, stay_high, leave_low, leave_high = project_other(
        place, other, query_weight, down, query_mine, rank_mine, slots, owned, up
    )

    received_high, received_low = swap(leave_high, 1), swap(leave_low, 1)
    place, _ = lax.optimization_barrier((place, leave_high))
    output_weight = dequantize_all(place, output_quant_codes, output_absmax_scale, True)
    received_high, _ = lax.optimization_barrier((received_high, output_weight))
    received_low, _ = lax.optimization_barrier((received_low, output_weight))

    def blocks_of(array):
        return [array[at : at + rows_dev] for at in range(0, array.shape[0], rows_dev)]

    high_blocks = blocks_of(stay_high + received_high)
    middle = len(high_blocks)
    sums = [swap(part, offset) for part, offset in zip(high_blocks, far_offsets[middle - 1 :])]
    low_blocks = blocks_of(stay_low + received_low)
    sums += [swap(part, offset) for part, offset in zip(low_blocks[1:], far_offsets)]
    query_vector = sum(sums, low_blocks[0])

    context = attend(
        query_vector,
        row_cache_length,
        stored_key_cache,
        stored_value_cache,
        fresh_token_key,
        fresh_token_value,
    )
    arrived = [context] + [swap(context, offset) for offset in far_offsets[::-1]][::-1]
    low = jnp.concatenate(arrived, axis=0)
    high = jnp.concatenate([swap(part, 1) for part in arrived], axis=0)
    theirs = cross(project_out(low, high, output_weight, 0))
    mine = project_out(low, high, output_weight, 1)
    routed = lax.all_to_all(sum_halves(place, offsets, mine, theirs), ("wide", "tensor"), 0, 0)
    return join_columns(routed)


def solution(mesh):
    in_specs = (
        P(("rep", "wide"), None),
        P(None, ("tensor", "wide")),
        P(None, ("tensor", "wide")),
        P("tensor", "wide"),
        P("tensor", "wide"),
        P(None, "wide", None),
        P("wide", None, "tensor"),
        P("rep"),
        P(),
        P(("rep", "wide")),
        P(("rep", "wide"), None, "tensor"),
        P(("rep", "wide"), None, "tensor"),
        P(("rep", "wide"), "tensor"),
        P(("rep", "wide"), "tensor"),
    )
    out_specs = P(("rep", "wide"), None)
    wide = mesh.shape["wide"]

    def on_device(*args):
        query_width, out_width = args[1].shape[1], args[3].shape[1]
        whole_tiles = query_width % LANES == 0 and out_width % (2 * LANES) == 0
        return fast(wide, *args) if whole_tiles else plain(*args)

    return jax.shard_map(
        on_device, mesh=mesh, in_specs=in_specs, out_specs=out_specs, check_vma=False
    )
```

```python
import math

import jax
import jax.numpy as jnp
import numpy as np
from jax import lax
from jax.experimental import pallas as pl
from jax.experimental.pallas import tpu as pltpu
from jax.sharding import PartitionSpec as P

HEAD_SIZE = 128
QBLOCK = 64
LANES = 128


NF4_LEVELS = (
    -1.0,
    -0.6961928009986877,
    -0.5250730514526367,
    -0.39491748809814453,
    -0.28444138169288635,
    -0.18477343022823334,
    -0.09105003625154495,
    0.0,
    0.07958029955625534,
    0.16093020141124725,
    0.24611230194568634,
    0.33791524171829224,
    0.44070982933044434,
    0.5626170039176941,
    0.7229568362236023,
    1.0,
)
ADAPTER_SCALE = 0.5
NEG_LARGE = -1e30
MIB = 1 << 20
VMEM = pl.BlockSpec(memory_space=pltpu.VMEM)
SMEM = pl.BlockSpec(memory_space=pltpu.SMEM)
ANY = pl.BlockSpec(memory_space=pl.ANY)
LOOKUP = lax.GatherDimensionNumbers(
    offset_dims=(),
    collapsed_slice_dims=(0,),
    start_index_map=(0,),
    operand_batching_dims=(1,),
    start_indices_batching_dims=(1,),
)


def dequantize(codes, scales):
    levels = jnp.zeros(codes.shape, jnp.float32)
    for number, level in enumerate(NF4_LEVELS):
        levels = jnp.where(codes == number, level, levels)
    height, breadth = codes.shape
    blocks = levels.reshape(height // QBLOCK, QBLOCK, breadth) * scales[:, None, :]
    return blocks.reshape(height, breadth).astype(jnp.bfloat16)


def dequantize_all(codes, scales, halves, *after):
    chunk = 512
    height, breadth = codes.shape
    blocks = chunk // QBLOCK
    parts = 2 if halves else 1
    width = breadth // parts

    def kernel(codes_ref, scales_ref, *rest):
        out_ref = rest[-1]
        core = lax.axis_index("tensor")
        number = lax.broadcasted_iota(jnp.int32, (16, LANES), 0)
        table = jnp.zeros((16, LANES), jnp.float32)
        for code, level in enumerate(NF4_LEVELS):
            table = jnp.where(number == code, level, table)

        def work(step, carry):
            for lane in range(0, breadth, LANES):
                part = lane // width
                place_in = (part + 1 + core) % 2 if halves else 0
                group = scales_ref[
                    pl.ds(pl.multiple_of(step * blocks, blocks), blocks), lane : lane + LANES
                ]
                for block in range(blocks):
                    products = (table * group[block : block + 1]).astype(jnp.bfloat16)
                    at = pl.multiple_of(step * chunk + block * QBLOCK, QBLOCK)
                    numbers = codes_ref[pl.ds(at, QBLOCK), lane : lane + LANES].astype(jnp.int16)
                    to = lane - part * width
                    for piece in range(0, QBLOCK, 16):
                        out_ref[place_in, pl.ds(at + piece, 16), to : to + LANES] = lax.gather(
                            products,
                            numbers[piece : piece + 16][..., None],
                            LOOKUP,
                            (1, 1),
                            mode=lax.GatherScatterMode.PROMISE_IN_BOUNDS,
                        )
            return carry

        lax.fori_loop(0, height // chunk, work, 0)

    return pl.pallas_call(
        kernel,
        in_specs=[VMEM, VMEM] + [ANY] * len(after),
        out_specs=VMEM,
        out_shape=pltpu.VMEM((parts, height, width), jnp.bfloat16),
        compiler_params=pltpu.CompilerParams(vmem_limit_bytes=2 * MIB),
        cost_estimate=pl.CostEstimate(
            flops=2 * height * breadth, bytes_accessed=6 * height * breadth, transcendentals=0
        ),
        name="dequantize",
    )(codes, scales, *after)


def begin_gather(block):
    def kernel(block_ref, out_ref):
        del block_ref, out_ref

    return pl.pallas_call(
        kernel,
        in_specs=[VMEM],
        out_specs=VMEM,
        out_shape=pltpu.VMEM(block.shape, block.dtype),
        input_output_aliases={0: 0},
        compiler_params=pltpu.CompilerParams(vmem_limit_bytes=2 * MIB),
        cost_estimate=pl.CostEstimate(
            flops=6_000_000_000, bytes_accessed=4 * block.size, transcendentals=0
        ),
        name="begin_gather",
    )(block)


LAST = (((1,), (1,)), ((), ()))


def find_slots(offsets, row_adapter_index, adapter_storage_slot, after):
    count = row_adapter_index.shape[0]
    block = count // len(offsets)

    def kernel(adapters_ref, storage_ref, after_ref, slots_ref):
        me = lax.axis_index("wide").astype(jnp.int32)
        column = lax.broadcasted_iota(jnp.int32, slots_ref.shape, 1)
        slots = jnp.zeros(slots_ref.shape, jnp.int32)
        for row in range(count):
            source = (me ^ int(offsets[row // block])) * block + row % block
            slots = jnp.where(column == row, storage_ref[adapters_ref[source]], slots)
        slots_ref[...] = slots

    return pl.pallas_call(
        kernel,
        in_specs=[SMEM, SMEM, ANY],
        out_specs=VMEM,
        out_shape=jax.ShapeDtypeStruct((8, count), jnp.int32),
        compiler_params=pltpu.CompilerParams(vmem_limit_bytes=2 * MIB),
        name="find_slots",
    )(row_adapter_index, adapter_storage_slot, after)


def project_own(own, weight, down):
    count = own[0].shape[0] * 2
    half = own[0].shape[1]
    query_width = weight.shape[2]

    def kernel(
        low,
        high,
        weight_ref,
        down_ref,
        query_ref,
        rank_ref,
    ):
        rows = jnp.concatenate([low[...], high[...]], axis=0)
        here = pl.ds(pl.multiple_of(lax.axis_index("tensor") * half, half), half)
        rank_ref[...] = lax.dot_general(
            down_ref[:, here], rows, LAST, preferred_element_type=jnp.float32
        )
        query_ref[...] = jnp.dot(rows, weight_ref[0, here], preferred_element_type=jnp.float32)

    return pl.pallas_call(
        kernel,
        in_specs=[VMEM] * 4,
        out_specs=[VMEM] * 2,
        out_shape=[
            jax.ShapeDtypeStruct((count, query_width), jnp.float32),
            jax.ShapeDtypeStruct((down.shape[0], count), jnp.float32),
        ],
        compiler_params=pltpu.CompilerParams(vmem_limit_bytes=4 * MIB),
        cost_estimate=pl.CostEstimate(
            flops=2 * count * half * (query_width + down.shape[0]),
            bytes_accessed=7 * MIB,
            transcendentals=0,
        ),
        name="project_own",
    )(*own, weight, down)


def project_other(other, weight, down, query_mine, rank_mine, slots, owned, up):
    count = other[0].shape[0] * 2
    half = other[0].shape[1]
    query_width = weight.shape[2]
    width = up.shape[1]
    rank = up.shape[0] // owned
    part = count // 4
    chunk = 512

    def kernel(
        low,
        high,
        weight_ref,
        down_ref,
        query_ref,
        rank_ref,
        slots_ref,
        up_ref,
        *out_refs,
    ):
        me = lax.axis_index("wide").astype(jnp.int32)
        rows = jnp.concatenate([low[...], high[...]], axis=0)
        there = pl.ds(pl.multiple_of((1 - lax.axis_index("tensor")) * half, half), half)
        ranks = rank_ref[...] + lax.dot_general(
            down_ref[:, there], rows, LAST, preferred_element_type=jnp.float32
        )
        slot = slots_ref[:1]
        kept = [
            jnp.where(slot == me * owned + number, ranks[at : at + rank], 0.0)
            for number, at in enumerate(range(0, owned * rank, rank))
        ]
        terms = jnp.concatenate(kept, axis=0).T.astype(jnp.bfloat16)
        query = query_ref[...] + jnp.dot(
            rows, weight_ref[0, there], preferred_element_type=jnp.float32
        )
        base = query.astype(jnp.bfloat16).astype(jnp.float32)
        for lane in range(0, width, chunk):
            delta = jnp.dot(
                terms, up_ref[:, lane : lane + chunk], preferred_element_type=jnp.float32
            ).astype(jnp.bfloat16)
            scaled = (ADAPTER_SCALE * delta.astype(jnp.float32)).astype(jnp.bfloat16)
            for number, out_ref in enumerate(out_refs):
                out_ref[:, lane : lane + chunk] = scaled[number * part : (number + 1) * part]
        here = pl.ds(pl.multiple_of(me * query_width, query_width), query_width)
        for number, out_ref in enumerate(out_refs):
            rows_base = base[number * part : (number + 1) * part]
            out_ref[:, here] = (rows_base + out_ref[:, here].astype(jnp.float32)).astype(
                jnp.bfloat16
            )

    shape = jax.ShapeDtypeStruct((part, width), jnp.bfloat16)
    return pl.pallas_call(
        kernel,
        in_specs=[VMEM] * 8,
        out_specs=[VMEM] * 4,
        out_shape=[shape] * 4,
        compiler_params=pltpu.CompilerParams(vmem_limit_bytes=4 * MIB),
        cost_estimate=pl.CostEstimate(
            flops=2 * count * (half * (query_width + up.shape[0]) + up.shape[0] * width),
            bytes_accessed=8 * MIB,
            transcendentals=0,
        ),
        name="project_other",
    )(*other, weight, down, query_mine, rank_mine, slots, up)


def project_out(low, high, weight, part):
    count = low.shape[0] * 2
    _, height, breadth = weight.shape

    def kernel(low_ref, high_ref, weight_ref, out_ref):
        rows = jnp.concatenate([low_ref[...], high_ref[...]], axis=0)
        out_ref[...] = jnp.dot(rows, weight_ref[part], preferred_element_type=jnp.float32)

    return pl.pallas_call(
        kernel,
        in_specs=[VMEM] * 3,
        out_specs=VMEM,
        out_shape=jax.ShapeDtypeStruct((count, breadth), jnp.float32),
        compiler_params=pltpu.CompilerParams(vmem_limit_bytes=4 * MIB),
        cost_estimate=pl.CostEstimate(
            flops=2 * count * height * breadth, bytes_accessed=6 * MIB, transcendentals=0
        ),
        name="project_out",
    )(low, high, weight)


def sum_halves(offsets, mine, theirs):
    block = 8
    count, width = mine.shape

    def kernel(mine_ref, theirs_ref, out_ref):
        me = lax.axis_index("wide").astype(jnp.int32)
        for number, at in enumerate(range(0, count, block)):
            rows = (mine_ref[at : at + block] + theirs_ref[at : at + block]).astype(jnp.bfloat16)
            for side in range(2):
                out_ref[(me ^ int(offsets[number])) * 2 + side] = rows

    return pl.pallas_call(
        kernel,
        in_specs=[VMEM, VMEM],
        out_specs=VMEM,
        out_shape=jax.ShapeDtypeStruct((count // block * 2, block, width), jnp.bfloat16),
        compiler_params=pltpu.CompilerParams(vmem_limit_bytes=4 * MIB),
        name="sum_halves",
    )(mine, theirs)


def join_columns(pieces):
    sources, rows, width = pieces.shape

    def kernel(pieces_ref, out_ref):
        for source in range(sources):
            out_ref[:, source * width : (source + 1) * width] = pieces_ref[source]

    return pl.pallas_call(
        kernel,
        in_specs=[VMEM],
        out_specs=VMEM,
        out_shape=jax.ShapeDtypeStruct((rows, sources * width), pieces.dtype),
        compiler_params=pltpu.CompilerParams(vmem_limit_bytes=4 * MIB),
        name="join_columns",
    )(pieces)


def attend(
    query_vector,
    row_cache_length,
    stored_key_cache,
    stored_value_cache,
    fresh_token_key,
    fresh_token_value,
):
    rows_dev = query_vector.shape[0]
    kv_local = stored_key_cache.shape[2] // HEAD_SIZE
    length = stored_key_cache.shape[1]
    grouped = query_vector.reshape(rows_dev, kv_local, -1, HEAD_SIZE)
    keys = stored_key_cache.reshape(rows_dev, length, kv_local, HEAD_SIZE)
    values = stored_value_cache.reshape(rows_dev, length, kv_local, HEAD_SIZE)
    scores = jnp.einsum(
        "rgkd,rtgd->rgkt", grouped, keys, preferred_element_type=jnp.float32
    ) / math.sqrt(HEAD_SIZE)
    valid = jnp.arange(length)[None, :] < row_cache_length[:, None]
    scores = jnp.where(valid[:, None, None, :], scores, NEG_LARGE)
    fresh = jnp.einsum(
        "rgkd,rgd->rgk",
        grouped,
        fresh_token_key.reshape(rows_dev, kv_local, HEAD_SIZE),
        preferred_element_type=jnp.float32,
    ) / math.sqrt(HEAD_SIZE)
    highest = jnp.maximum(jnp.max(scores, axis=-1), fresh)
    weights = jnp.exp(scores - highest[..., None])
    fresh_weight = jnp.exp(fresh - highest)
    total = jnp.sum(weights, axis=-1) + fresh_weight
    probs = (weights / total[..., None]).astype(jnp.bfloat16)
    fresh_prob = (fresh_weight / total).astype(jnp.bfloat16)
    context = jnp.einsum("rgkt,rtgd->rgkd", probs, values, preferred_element_type=jnp.float32)
    context = context + fresh_prob.astype(jnp.float32)[..., None] * fresh_token_value.reshape(
        rows_dev, kv_local, 1, HEAD_SIZE
    ).astype(jnp.float32)
    return context.astype(jnp.bfloat16).reshape(
        rows_dev, kv_local * grouped.shape[2] * HEAD_SIZE
    )


def plain(
    tokens,
    query_quant_codes,
    query_absmax_scale,
    output_quant_codes,
    output_absmax_scale,
    adapter_down_maps,
    adapter_up_maps,
    row_adapter_index,
    adapter_storage_slot,
    row_cache_length,
    stored_key_cache,
    stored_value_cache,
    fresh_token_key,
    fresh_token_value,
):
    query_weight = dequantize(query_quant_codes, query_absmax_scale)
    query_width = query_weight.shape[1]
    owned_portion = adapter_down_maps.shape[1]
    adapter_rank_size = adapter_down_maps.shape[2]
    down_matrix_flat = adapter_down_maps.reshape(
        adapter_down_maps.shape[0], owned_portion * adapter_rank_size
    )
    joined = jnp.concatenate([query_weight, down_matrix_flat], axis=1)
    projected = jnp.dot(
        lax.all_gather(tokens, "wide", axis=0, tiled=True),
        joined,
        preferred_element_type=jnp.float32,
    )
    query_base = projected[:, :query_width].astype(jnp.bfloat16)
    down_all = projected[:, query_width:]
    matches = row_adapter_index[:, None] == jnp.arange(adapter_storage_slot.shape[0])[None, :]
    slots = jnp.sum(jnp.where(matches, adapter_storage_slot[None, :], 0), axis=1)
    local_slot = slots - lax.axis_index("wide") * owned_portion
    query_transferred = lax.all_to_all(query_base, "wide", split_axis=0, concat_axis=1, tiled=True)
    column_owner = jnp.arange(owned_portion * adapter_rank_size) // adapter_rank_size
    keep = column_owner[None, :] == local_slot[:, None]
    rank_terms = jnp.where(keep, down_all, 0.0).astype(jnp.bfloat16)
    up_matrix_flat = adapter_up_maps.reshape(
        owned_portion * adapter_rank_size, adapter_up_maps.shape[2]
    )
    rounded = jnp.dot(rank_terms, up_matrix_flat, preferred_element_type=jnp.float32).astype(
        jnp.bfloat16
    )
    adapter_update = lax.psum_scatter(
        lax.optimization_barrier(rounded).astype(jnp.float32),
        "wide",
        scatter_dimension=0,
        tiled=True,
    )
    query_vector = (query_transferred.astype(jnp.float32) + ADAPTER_SCALE * adapter_update).astype(
        jnp.bfloat16
    )
    context = attend(
        query_vector,
        row_cache_length,
        stored_key_cache,
        stored_value_cache,
        fresh_token_key,
        fresh_token_value,
    )
    output_weight = dequantize(output_quant_codes, output_absmax_scale)
    partial_out = jnp.dot(
        lax.all_gather(context, "wide", axis=0, tiled=True),
        output_weight,
        preferred_element_type=jnp.float32,
    )
    summed = lax.psum(partial_out, "tensor")
    routed = lax.all_to_all(
        summed.astype(jnp.bfloat16), "wide", split_axis=0, concat_axis=1, tiled=True
    )
    return routed


def fast(
    wide,
    tokens,
    query_quant_codes,
    query_absmax_scale,
    output_quant_codes,
    output_absmax_scale,
    adapter_down_maps,
    adapter_up_maps,
    row_adapter_index,
    adapter_storage_slot,
    row_cache_length,
    stored_key_cache,
    stored_value_cache,
    fresh_token_key,
    fresh_token_value,
):
    rows_dev, model_width = tokens.shape
    half = model_width // 2
    offsets = np.array([far * 2 + near for near in range(2) for far in range(wide // 2)], np.int32)

    core = lax.axis_index("tensor").astype(jnp.int32)

    def swap(array, offset):
        return lax.ppermute(array, "wide", [(peer, peer ^ offset) for peer in range(wide)])

    def cross(array):
        return lax.ppermute(array, "tensor", [(0, 1), (1, 0)])

    far_offsets = range(2, wide, 2)

    block = lax.dynamic_slice(tokens, (0, core * half), (rows_dev, half))
    block = begin_gather(block)
    blocks = [block] + [swap(block, offset) for offset in far_offsets]
    query_weight = dequantize_all(query_quant_codes, query_absmax_scale, False, block)
    blocks[1:] = [lax.optimization_barrier((part, query_weight))[0] for part in blocks[1:]]
    low = jnp.concatenate(blocks, axis=0)
    nearby = [swap(part, 1) for part in blocks]
    slots = find_slots(offsets, row_adapter_index, adapter_storage_slot, low)
    nearby = [lax.optimization_barrier((part, slots))[0] for part in nearby]
    high = jnp.concatenate(nearby, axis=0)
    own = (low, high)
    other = [cross(part) for part in own]

    owned, rank = adapter_down_maps.shape[1:]
    down = adapter_down_maps.transpose(1, 2, 0).reshape(owned * rank, model_width)
    up = adapter_up_maps.reshape(owned * rank, adapter_up_maps.shape[2])
    query_mine, rank_mine = project_own(own, query_weight, down)
    stay_low, stay_high, leave_low, leave_high = project_other(
        other, query_weight, down, query_mine, rank_mine, slots, owned, up
    )

    received_high, received_low = swap(leave_high, 1), swap(leave_low, 1)
    output_weight = dequantize_all(output_quant_codes, output_absmax_scale, True, leave_high)
    received_high, _ = lax.optimization_barrier((received_high, output_weight))
    received_low, _ = lax.optimization_barrier((received_low, output_weight))

    def blocks_of(array):
        return [array[at : at + rows_dev] for at in range(0, array.shape[0], rows_dev)]

    high_blocks = blocks_of(stay_high + received_high)
    middle = len(high_blocks)
    sums = [swap(part, offset) for part, offset in zip(high_blocks, far_offsets[middle - 1 :])]
    low_blocks = blocks_of(stay_low + received_low)
    sums += [swap(part, offset) for part, offset in zip(low_blocks[1:], far_offsets)]
    query_vector = sum(sums, low_blocks[0])

    context = attend(
        query_vector,
        row_cache_length,
        stored_key_cache,
        stored_value_cache,
        fresh_token_key,
        fresh_token_value,
    )
    arrived = [context] + [swap(context, offset) for offset in far_offsets[::-1]][::-1]
    low = jnp.concatenate(arrived, axis=0)
    high = jnp.concatenate([swap(part, 1) for part in arrived], axis=0)
    theirs = cross(project_out(low, high, output_weight, 0))
    mine = project_out(low, high, output_weight, 1)
    routed = lax.all_to_all(sum_halves(offsets, mine, theirs), ("wide", "tensor"), 0, 0)
    return join_columns(routed)


def solution(mesh):
    in_specs = (
        P(("rep", "wide"), None),
        P(None, ("tensor", "wide")),
        P(None, ("tensor", "wide")),
        P("tensor", "wide"),
        P("tensor", "wide"),
        P(None, "wide", None),
        P("wide", None, "tensor"),
        P("rep"),
        P(),
        P(("rep", "wide")),
        P(("rep", "wide"), None, "tensor"),
        P(("rep", "wide"), None, "tensor"),
        P(("rep", "wide"), "tensor"),
        P(("rep", "wide"), "tensor"),
    )
    out_specs = P(("rep", "wide"), None)
    wide = mesh.shape["wide"]

    def on_device(*args):
        query_width, out_width = args[1].shape[1], args[3].shape[1]
        whole_tiles = query_width % LANES == 0 and out_width % (2 * LANES) == 0
        return fast(wide, *args) if whole_tiles else plain(*args)

    return jax.shard_map(
        on_device, mesh=mesh, in_specs=in_specs, out_specs=out_specs, check_vma=False
    )
```

```python
import math

import jax
import jax.numpy as jnp
import numpy as np
from jax import lax
from jax.experimental import pallas as pl
from jax.experimental.pallas import tpu as pltpu
from jax.sharding import PartitionSpec as P

HEAD_SIZE = 128
QBLOCK = 64
LANES = 128


NF4_LEVELS = (
    -1.0,
    -0.6961928009986877,
    -0.5250730514526367,
    -0.39491748809814453,
    -0.28444138169288635,
    -0.18477343022823334,
    -0.09105003625154495,
    0.0,
    0.07958029955625534,
    0.16093020141124725,
    0.24611230194568634,
    0.33791524171829224,
    0.44070982933044434,
    0.5626170039176941,
    0.7229568362236023,
    1.0,
)
ADAPTER_SCALE = 0.5
NEG_LARGE = -1e30
MIB = 1 << 20
VMEM = pl.BlockSpec(memory_space=pltpu.VMEM)
SMEM = pl.BlockSpec(memory_space=pltpu.SMEM)
ANY = pl.BlockSpec(memory_space=pl.ANY)
LOOKUP = lax.GatherDimensionNumbers(
    offset_dims=(),
    collapsed_slice_dims=(0,),
    start_index_map=(0,),
    operand_batching_dims=(1,),
    start_indices_batching_dims=(1,),
)


def dequantize(codes, scales):
    levels = jnp.zeros(codes.shape, jnp.float32)
    for number, level in enumerate(NF4_LEVELS):
        levels = jnp.where(codes == number, level, levels)
    height, breadth = codes.shape
    blocks = levels.reshape(height // QBLOCK, QBLOCK, breadth) * scales[:, None, :]
    return blocks.reshape(height, breadth).astype(jnp.bfloat16)


def dequantize_all(codes, scales, halves, *after):
    chunk = 512
    height, breadth = codes.shape
    blocks = chunk // QBLOCK
    parts = 2 if halves else 1
    width = breadth // parts

    def kernel(codes_ref, scales_ref, *rest):
        out_ref = rest[-1]
        core = lax.axis_index("tensor")
        number = lax.broadcasted_iota(jnp.int32, (16, LANES), 0)
        table = jnp.zeros((16, LANES), jnp.float32)
        for code, level in enumerate(NF4_LEVELS):
            table = jnp.where(number == code, level, table)

        def work(step, carry):
            for lane in range(0, breadth, LANES):
                part = lane // width
                place_in = (part + 1 + core) % 2 if halves else 0
                group = scales_ref[
                    pl.ds(pl.multiple_of(step * blocks, blocks), blocks), lane : lane + LANES
                ]
                for block in range(blocks):
                    products = (table * group[block : block + 1]).astype(jnp.bfloat16)
                    at = pl.multiple_of(step * chunk + block * QBLOCK, QBLOCK)
                    numbers = codes_ref[pl.ds(at, QBLOCK), lane : lane + LANES].astype(jnp.int16)
                    to = lane - part * width
                    for piece in range(0, QBLOCK, 16):
                        out_ref[place_in, pl.ds(at + piece, 16), to : to + LANES] = lax.gather(
                            products,
                            numbers[piece : piece + 16][..., None],
                            LOOKUP,
                            (1, 1),
                            mode=lax.GatherScatterMode.PROMISE_IN_BOUNDS,
                        )
            return carry

        lax.fori_loop(0, height // chunk, work, 0)

    return pl.pallas_call(
        kernel,
        in_specs=[VMEM, VMEM] + [ANY] * len(after),
        out_specs=VMEM,
        out_shape=pltpu.VMEM((parts, height, width), jnp.bfloat16),
        compiler_params=pltpu.CompilerParams(vmem_limit_bytes=2 * MIB),
        cost_estimate=pl.CostEstimate(
            flops=2 * height * breadth, bytes_accessed=6 * height * breadth, transcendentals=0
        ),
        name="dequantize",
    )(codes, scales, *after)


def begin_gather(block):
    def kernel(block_ref, out_ref):
        del block_ref, out_ref

    return pl.pallas_call(
        kernel,
        in_specs=[VMEM],
        out_specs=VMEM,
        out_shape=pltpu.VMEM(block.shape, block.dtype),
        input_output_aliases={0: 0},
        compiler_params=pltpu.CompilerParams(vmem_limit_bytes=2 * MIB),
        cost_estimate=pl.CostEstimate(
            flops=6_000_000_000, bytes_accessed=4 * block.size, transcendentals=0
        ),
        name="begin_gather",
    )(block)


LAST = (((1,), (1,)), ((), ()))


def find_slots(offsets, row_adapter_index, adapter_storage_slot, after):
    count = row_adapter_index.shape[0]
    block = count // len(offsets)

    def kernel(adapters_ref, storage_ref, after_ref, slots_ref):
        me = lax.axis_index("wide").astype(jnp.int32)
        column = lax.broadcasted_iota(jnp.int32, slots_ref.shape, 1)
        slots = jnp.zeros(slots_ref.shape, jnp.int32)
        for row in range(count):
            source = (me ^ int(offsets[row // block])) * block + row % block
            slots = jnp.where(column == row, storage_ref[adapters_ref[source]], slots)
        slots_ref[...] = slots

    return pl.pallas_call(
        kernel,
        in_specs=[SMEM, SMEM, ANY],
        out_specs=VMEM,
        out_shape=jax.ShapeDtypeStruct((8, count), jnp.int32),
        compiler_params=pltpu.CompilerParams(vmem_limit_bytes=2 * MIB),
        name="find_slots",
    )(row_adapter_index, adapter_storage_slot, after)


def project_own(own, weight, down):
    count = own[0].shape[0] * 2
    half = own[0].shape[1]
    query_width = weight.shape[2]

    def kernel(
        low,
        high,
        weight_ref,
        down_ref,
        query_ref,
        rank_ref,
    ):
        rows = jnp.concatenate([low[...], high[...]], axis=0)
        here = pl.ds(pl.multiple_of(lax.axis_index("tensor") * half, half), half)
        rank_ref[...] = lax.dot_general(
            down_ref[:, here], rows, LAST, preferred_element_type=jnp.float32
        )
        query_ref[...] = jnp.dot(rows, weight_ref[0, here], preferred_element_type=jnp.float32)

    return pl.pallas_call(
        kernel,
        in_specs=[VMEM] * 4,
        out_specs=[VMEM] * 2,
        out_shape=[
            jax.ShapeDtypeStruct((count, query_width), jnp.float32),
            jax.ShapeDtypeStruct((down.shape[0], count), jnp.float32),
        ],
        compiler_params=pltpu.CompilerParams(vmem_limit_bytes=4 * MIB),
        cost_estimate=pl.CostEstimate(
            flops=2 * count * half * (query_width + down.shape[0]),
            bytes_accessed=7 * MIB,
            transcendentals=0,
        ),
        name="project_own",
    )(*own, weight, down)


def project_other(other, weight, down, query_mine, rank_mine, slots, owned, up):
    count = other[0].shape[0] * 2
    half = other[0].shape[1]
    query_width = weight.shape[2]
    width = up.shape[1]
    rank = up.shape[0] // owned
    part = count // 4
    chunk = 512

    def kernel(
        low,
        high,
        weight_ref,
        down_ref,
        query_ref,
        rank_ref,
        slots_ref,
        up_ref,
        *out_refs,
    ):
        me = lax.axis_index("wide").astype(jnp.int32)
        rows = jnp.concatenate([low[...], high[...]], axis=0)
        there = pl.ds(pl.multiple_of((1 - lax.axis_index("tensor")) * half, half), half)
        ranks = rank_ref[...] + lax.dot_general(
            down_ref[:, there], rows, LAST, preferred_element_type=jnp.float32
        )
        slot = slots_ref[:1]
        kept = [
            jnp.where(slot == me * owned + number, ranks[at : at + rank], 0.0)
            for number, at in enumerate(range(0, owned * rank, rank))
        ]
        terms = jnp.concatenate(kept, axis=0).T.astype(jnp.bfloat16)
        query = query_ref[...] + jnp.dot(
            rows, weight_ref[0, there], preferred_element_type=jnp.float32
        )
        base = query.astype(jnp.bfloat16).astype(jnp.float32)
        for lane in range(0, width, chunk):
            delta = jnp.dot(
                terms, up_ref[:, lane : lane + chunk], preferred_element_type=jnp.float32
            ).astype(jnp.bfloat16)
            scaled = (ADAPTER_SCALE * delta.astype(jnp.float32)).astype(jnp.bfloat16)
            for number, out_ref in enumerate(out_refs):
                out_ref[:, lane : lane + chunk] = scaled[number * part : (number + 1) * part]
        here = pl.ds(pl.multiple_of(me * query_width, query_width), query_width)
        for number, out_ref in enumerate(out_refs):
            rows_base = base[number * part : (number + 1) * part]
            out_ref[:, here] = (rows_base + out_ref[:, here].astype(jnp.float32)).astype(
                jnp.bfloat16
            )

    shape = jax.ShapeDtypeStruct((part, width), jnp.bfloat16)
    return pl.pallas_call(
        kernel,
        in_specs=[VMEM] * 8,
        out_specs=[VMEM] * 4,
        out_shape=[shape] * 4,
        compiler_params=pltpu.CompilerParams(vmem_limit_bytes=4 * MIB),
        cost_estimate=pl.CostEstimate(
            flops=2 * count * (half * (query_width + up.shape[0]) + up.shape[0] * width),
            bytes_accessed=8 * MIB,
            transcendentals=0,
        ),
        name="project_other",
    )(*other, weight, down, query_mine, rank_mine, slots, up)


def project_out(low, high, weight, part):
    count = low.shape[0] * 2
    _, height, breadth = weight.shape

    def kernel(low_ref, high_ref, weight_ref, out_ref):
        rows = jnp.concatenate([low_ref[...], high_ref[...]], axis=0)
        out_ref[...] = jnp.dot(rows, weight_ref[part], preferred_element_type=jnp.float32)

    return pl.pallas_call(
        kernel,
        in_specs=[VMEM] * 3,
        out_specs=VMEM,
        out_shape=jax.ShapeDtypeStruct((count, breadth), jnp.float32),
        compiler_params=pltpu.CompilerParams(vmem_limit_bytes=4 * MIB),
        cost_estimate=pl.CostEstimate(
            flops=2 * count * height * breadth, bytes_accessed=6 * MIB, transcendentals=0
        ),
        name="project_out",
    )(low, high, weight)


def sum_halves(offsets, mine, theirs):
    block = 8
    count, width = mine.shape

    def kernel(mine_ref, theirs_ref, out_ref):
        me = lax.axis_index("wide").astype(jnp.int32)
        for number, at in enumerate(range(0, count, block)):
            rows = (mine_ref[at : at + block] + theirs_ref[at : at + block]).astype(jnp.bfloat16)
            for side in range(2):
                out_ref[(me ^ int(offsets[number])) * 2 + side] = rows

    return pl.pallas_call(
        kernel,
        in_specs=[VMEM, VMEM],
        out_specs=VMEM,
        out_shape=jax.ShapeDtypeStruct((count // block * 2, block, width), jnp.bfloat16),
        compiler_params=pltpu.CompilerParams(vmem_limit_bytes=4 * MIB),
        name="sum_halves",
    )(mine, theirs)


def join_columns(pieces):
    sources, rows, width = pieces.shape

    def kernel(pieces_ref, out_ref):
        for source in range(sources):
            out_ref[:, source * width : (source + 1) * width] = pieces_ref[source]

    return pl.pallas_call(
        kernel,
        in_specs=[VMEM],
        out_specs=VMEM,
        out_shape=jax.ShapeDtypeStruct((rows, sources * width), pieces.dtype),
        compiler_params=pltpu.CompilerParams(vmem_limit_bytes=4 * MIB),
        name="join_columns",
    )(pieces)


def attend(
    query_vector,
    row_cache_length,
    stored_key_cache,
    stored_value_cache,
    fresh_token_key,
    fresh_token_value,
):
    rows_dev = query_vector.shape[0]
    kv_local = stored_key_cache.shape[2] // HEAD_SIZE
    length = stored_key_cache.shape[1]
    grouped = query_vector.reshape(rows_dev, kv_local, -1, HEAD_SIZE)
    keys = stored_key_cache.reshape(rows_dev, length, kv_local, HEAD_SIZE)
    values = stored_value_cache.reshape(rows_dev, length, kv_local, HEAD_SIZE)
    scores = jnp.einsum(
        "rgkd,rtgd->rgkt", grouped, keys, preferred_element_type=jnp.float32
    ) / math.sqrt(HEAD_SIZE)
    valid = jnp.arange(length)[None, :] < row_cache_length[:, None]
    scores = jnp.where(valid[:, None, None, :], scores, NEG_LARGE)
    fresh = jnp.einsum(
        "rgkd,rgd->rgk",
        grouped,
        fresh_token_key.reshape(rows_dev, kv_local, HEAD_SIZE),
        preferred_element_type=jnp.float32,
    ) / math.sqrt(HEAD_SIZE)
    highest = jnp.maximum(jnp.max(scores, axis=-1), fresh)
    weights = jnp.exp(scores - highest[..., None])
    fresh_weight = jnp.exp(fresh - highest)
    total = jnp.sum(weights, axis=-1) + fresh_weight
    probs = (weights / total[..., None]).astype(jnp.bfloat16)
    fresh_prob = (fresh_weight / total).astype(jnp.bfloat16)
    context = jnp.einsum("rgkt,rtgd->rgkd", probs, values, preferred_element_type=jnp.float32)
    context = context + fresh_prob.astype(jnp.float32)[..., None] * fresh_token_value.reshape(
        rows_dev, kv_local, 1, HEAD_SIZE
    ).astype(jnp.float32)
    return context.astype(jnp.bfloat16).reshape(
        rows_dev, kv_local * grouped.shape[2] * HEAD_SIZE
    )


def plain(
    tokens,
    query_quant_codes,
    query_absmax_scale,
    output_quant_codes,
    output_absmax_scale,
    adapter_down_maps,
    adapter_up_maps,
    row_adapter_index,
    adapter_storage_slot,
    row_cache_length,
    stored_key_cache,
    stored_value_cache,
    fresh_token_key,
    fresh_token_value,
):
    query_weight = dequantize(query_quant_codes, query_absmax_scale)
    query_width = query_weight.shape[1]
    owned_portion = adapter_down_maps.shape[1]
    adapter_rank_size = adapter_down_maps.shape[2]
    down_matrix_flat = adapter_down_maps.reshape(
        adapter_down_maps.shape[0], owned_portion * adapter_rank_size
    )
    joined = jnp.concatenate([query_weight, down_matrix_flat], axis=1)
    projected = jnp.dot(
        lax.all_gather(tokens, "wide", axis=0, tiled=True),
        joined,
        preferred_element_type=jnp.float32,
    )
    query_base = projected[:, :query_width].astype(jnp.bfloat16)
    down_all = projected[:, query_width:]
    matches = row_adapter_index[:, None] == jnp.arange(adapter_storage_slot.shape[0])[None, :]
    slots = jnp.sum(jnp.where(matches, adapter_storage_slot[None, :], 0), axis=1)
    local_slot = slots - lax.axis_index("wide") * owned_portion
    query_transferred = lax.all_to_all(query_base, "wide", split_axis=0, concat_axis=1, tiled=True)
    column_owner = jnp.arange(owned_portion * adapter_rank_size) // adapter_rank_size
    keep = column_owner[None, :] == local_slot[:, None]
    rank_terms = jnp.where(keep, down_all, 0.0).astype(jnp.bfloat16)
    up_matrix_flat = adapter_up_maps.reshape(
        owned_portion * adapter_rank_size, adapter_up_maps.shape[2]
    )
    rounded = jnp.dot(rank_terms, up_matrix_flat, preferred_element_type=jnp.float32).astype(
        jnp.bfloat16
    )
    adapter_update = lax.psum_scatter(
        lax.optimization_barrier(rounded).astype(jnp.float32),
        "wide",
        scatter_dimension=0,
        tiled=True,
    )
    query_vector = (query_transferred.astype(jnp.float32) + ADAPTER_SCALE * adapter_update).astype(
        jnp.bfloat16
    )
    context = attend(
        query_vector,
        row_cache_length,
        stored_key_cache,
        stored_value_cache,
        fresh_token_key,
        fresh_token_value,
    )
    output_weight = dequantize(output_quant_codes, output_absmax_scale)
    partial_out = jnp.dot(
        lax.all_gather(context, "wide", axis=0, tiled=True),
        output_weight,
        preferred_element_type=jnp.float32,
    )
    summed = lax.psum(partial_out, "tensor")
    routed = lax.all_to_all(
        summed.astype(jnp.bfloat16), "wide", split_axis=0, concat_axis=1, tiled=True
    )
    return routed


def fast(
    wide,
    tokens,
    query_quant_codes,
    query_absmax_scale,
    output_quant_codes,
    output_absmax_scale,
    adapter_down_maps,
    adapter_up_maps,
    row_adapter_index,
    adapter_storage_slot,
    row_cache_length,
    stored_key_cache,
    stored_value_cache,
    fresh_token_key,
    fresh_token_value,
):
    rows_dev, model_width = tokens.shape
    half = model_width // 2
    offsets = np.array([far * 2 + near for near in range(2) for far in range(wide // 2)], np.int32)

    core = lax.axis_index("tensor").astype(jnp.int32)

    def swap(array, offset):
        return lax.ppermute(array, "wide", [(peer, peer ^ offset) for peer in range(wide)])

    def cross(array):
        return lax.ppermute(array, "tensor", [(0, 1), (1, 0)])

    far_offsets = range(2, wide, 2)

    block = lax.dynamic_slice(tokens, (0, core * half), (rows_dev, half))
    block = begin_gather(block)
    blocks = [block] + [swap(block, offset) for offset in far_offsets]
    query_weight = dequantize_all(query_quant_codes, query_absmax_scale, False, block)
    blocks[1:] = [lax.optimization_barrier((part, query_weight))[0] for part in blocks[1:]]
    low = jnp.concatenate(blocks, axis=0)
    nearby = [swap(part, 1) for part in blocks]
    slots = find_slots(offsets, row_adapter_index, adapter_storage_slot, low)
    nearby = [lax.optimization_barrier((part, slots))[0] for part in nearby]
    high = jnp.concatenate(nearby, axis=0)
    own = (low, high)
    other = [cross(part) for part in own]

    owned, rank = adapter_down_maps.shape[1:]
    down = adapter_down_maps.transpose(1, 2, 0).reshape(owned * rank, model_width)
    up = adapter_up_maps.reshape(owned * rank, adapter_up_maps.shape[2])
    query_mine, rank_mine = project_own(own, query_weight, down)
    stay_low, stay_high, leave_low, leave_high = project_other(
        other, query_weight, down, query_mine, rank_mine, slots, owned, up
    )

    received_high, received_low = swap(leave_high, 1), swap(leave_low, 1)
    output_weight = dequantize_all(
        output_quant_codes,
        output_absmax_scale,
        True,
        leave_high,
        stored_key_cache,
        stored_value_cache,
    )
    received_high, _ = lax.optimization_barrier((received_high, output_weight))
    received_low, _ = lax.optimization_barrier((received_low, output_weight))

    def blocks_of(array):
        return [array[at : at + rows_dev] for at in range(0, array.shape[0], rows_dev)]

    high_blocks = blocks_of(stay_high + received_high)
    middle = len(high_blocks)
    sums = [swap(part, offset) for part, offset in zip(high_blocks, far_offsets[middle - 1 :])]
    low_blocks = blocks_of(stay_low + received_low)
    sums += [swap(part, offset) for part, offset in zip(low_blocks[1:], far_offsets)]
    query_vector = sum(sums, low_blocks[0])

    context = attend(
        query_vector,
        row_cache_length,
        stored_key_cache,
        stored_value_cache,
        fresh_token_key,
        fresh_token_value,
    )
    arrived = [context] + [swap(context, offset) for offset in far_offsets[::-1]][::-1]
    low = jnp.concatenate(arrived, axis=0)
    high = jnp.concatenate([swap(part, 1) for part in arrived], axis=0)
    theirs = cross(project_out(low, high, output_weight, 0))
    mine = project_out(low, high, output_weight, 1)
    routed = lax.all_to_all(sum_halves(offsets, mine, theirs), ("wide", "tensor"), 0, 0)
    return join_columns(routed)


def solution(mesh):
    in_specs = (
        P(("rep", "wide"), None),
        P(None, ("tensor", "wide")),
        P(None, ("tensor", "wide")),
        P("tensor", "wide"),
        P("tensor", "wide"),
        P(None, "wide", None),
        P("wide", None, "tensor"),
        P("rep"),
        P(),
        P(("rep", "wide")),
        P(("rep", "wide"), None, "tensor"),
        P(("rep", "wide"), None, "tensor"),
        P(("rep", "wide"), "tensor"),
        P(("rep", "wide"), "tensor"),
    )
    out_specs = P(("rep", "wide"), None)
    wide = mesh.shape["wide"]

    def on_device(*args):
        query_width, out_width = args[1].shape[1], args[3].shape[1]
        whole_tiles = query_width % LANES == 0 and out_width % (2 * LANES) == 0
        return fast(wide, *args) if whole_tiles else plain(*args)

    return jax.shard_map(
        on_device, mesh=mesh, in_specs=in_specs, out_specs=out_specs, check_vma=False
    )
```
